128 devices in a mesh: expert: 32 (over x_lo, y, z), tensor: 4 (over x_hi, core).
Axes of the slice: x: 4 (x_hi: 2, x_lo: 2; x = x_hi * 2 + x_lo), y: 4, z: 4, core: 2. Of those that a mesh axis runs over, the one named last changes fastest.
Arguments:
- tokens: bfloat16 [4096, 3584], P('expert'), may hold values from -6 to 6
- norm_gain: float32 [3584], replicated, may hold values from 0.25 to 1.75
- router: bfloat16 [3584, 32], replicated, may hold values from -0.09375 to 0.09375
- expert_gate: bfloat16 [32, 3584, 2560], P('expert', None, 'tensor'), may hold values from -0.09375 to 0.09375
- expert_up: bfloat16 [32, 3584, 2560], P('expert', None, 'tensor'), may hold values from -0.09375 to 0.09375
- expert_down: bfloat16 [32, 2560, 3584], P('expert', 'tensor'), may hold values from -0.125 to 0.125
- dense_gate: bfloat16 [3584, 2560], P('expert', 'tensor'), may hold values from -0.09375 to 0.09375
- dense_up: bfloat16 [3584, 2560], P('expert', 'tensor'), may hold values from -0.09375 to 0.09375
- dense_down_t: bfloat16 [3584, 2560], P('expert', 'tensor'), may hold values from -0.125 to 0.125
- routes: int32 [4096, 2], P('expert'), may hold values from 0 to 31, all different within a row; in each aligned block of 128 rows (0 to 127, 128 to 255, ...) at most 12 rows name the same one
- grad_out: bfloat16 [4096, 3584], P('expert'), may hold values from -6 to 6
Outputs:
- layer_out: bfloat16 [4096, 3584], P('expert')
- grad_in: bfloat16 [4096, 3584], P('expert')
The draws below stay inside these ranges and needn't reach their ends.
Inputs may be any that keep to these rules, and one draw needn't show every extreme that they name: Among the 128 rows of each block no expert is named by more than 12 routes, a bound that some block reaches; the two experts of a row differ.
All inputs are finite; a program needn't handle non-finite values.
Results may differ from the reference program's by a relative error of at most 0.0055.
Values may be sent and summed in bfloat16 or wider, within the bound.
No kernel may reach another device: no remote copies, remote signals or barrier semaphores. Data moves between devices by JAX's collectives and lax.ppermute only.
A program may use at most 192 MiB of HBM per device.

```python
import math
import jax
import jax.numpy as jnp
import numpy as np
from jax import lax

D = 3584
EH = 2560
DH = 2560
TOK = 128
EXPERTS = 32
CAP = 12
TOKENS = 4096
N_EXPERT = 32


def block_scale(own_key, dims, cuts, smallest, top_value):
    def one(position, shards_of):
        heights = jax.random.uniform(jax.random.fold_in(jax.random.fold_in(own_key, 6), position), (shards_of,), jnp.float32, smallest / len(cuts), top_value / len(cuts))
        return jnp.repeat(jnp.exp(heights), dims[position] // shards_of).reshape((-1,) + (1,) * (len(dims) - position - 1))

    level = one(*cuts[0])
    for cut in cuts[1:]:
        level = level * one(*cut)
    return level


def deal_out(rng, own, number, rows, count, top, most, skew):
    ranking = jax.random.permutation(rng, count)
    crowded, usual = load_shares(count, rows * top, most, skew, True), load_shares(count, rows * top, most, skew, False)
    places = jnp.arange(count)

    def named(lengths, rotation):
        used = int((lengths > 0).sum())
        fixed = max(1, used // 4)
        passed = fixed + (places - fixed + rotation * (used - fixed)) % max(1, count - fixed)
        return jnp.zeros((count,), jnp.int32).at[ranking[jnp.where(places < fixed, places, passed)]].set(jnp.asarray(lengths, jnp.int32))

    lengths = jnp.where(number % 4 == 0, named(crowded, number // 4), named(usual, number - number // 4 - 1))
    mixed = jax.random.permutation(jax.random.fold_in(own, 3), count)
    giver, receiver = mixed[0:count // 2 * 2:2], mixed[1:count // 2 * 2:2]
    room = jnp.minimum(lengths[giver] - 1, most - lengths[receiver]) // 2
    room = jnp.where((giver == ranking[0]) | (receiver == ranking[0]) | (lengths[receiver] == 0), 0, jnp.maximum(room, 0))
    passed = jax.random.randint(jax.random.fold_in(own, 4), (count // 2,), 0, 1 << 20) % (room + 1)
    lengths = lengths.at[giver].add(-passed).at[receiver].add(passed)
    members = jnp.searchsorted(jnp.cumsum(lengths), jnp.arange(rows * top), side="right").astype(jnp.int32)
    grid = members.reshape(top, rows).T
    grid = grid[jax.random.permutation(jax.random.fold_in(own, 1), rows)]
    rotation = jax.random.randint(jax.random.fold_in(own, 2), (rows, 1), 0, top)
    return jnp.take_along_axis(grid, (jnp.arange(top)[None, :] + rotation) % top, axis=1)


def load_shares(amount, total, reach, lean, full):
    loads = [(1 << 20) // math.isqrt(rank ** lean) + 1 for rank in range(1, amount + 1)]
    largest = reach if full else min(reach, max(-(-total // amount), total * loads[0] // sum(loads)))
    least = 1 if total - largest >= amount - 1 else 0
    given, rest = [largest] + [least] * (amount - 1), total - largest - least * (amount - 1)
    while rest > 0:
        free = [i for i in range(1, amount) if given[i] < largest] or [i for i in range(1, amount) if given[i] < reach]
        mass, left = sum([loads[i] for i in free]), rest
        for i in free:
            addition = min(reach - given[i], max(1, left * loads[i] // mass), rest)
            given[i] = given[i] + addition
            rest = rest - addition
    return np.array(given)


def gaussian(own_key, dims, deviation, reach, split=(), held_as=jnp.bfloat16):
    entries = deviation * jax.random.normal(own_key, dims, jnp.float32)
    if split:
        entries = entries * block_scale(own_key, dims, split, -0.22, 0.18)
    return jnp.clip(entries, -reach, reach).astype(held_as)


def setup_inputs(seed: int = 0) -> dict:
    keys = jax.random.split(jax.random.key(seed), 12)
    tokens = gaussian(keys[0], (TOKENS, D), 1.0, 6.0, ((0, 32),))
    norm_gain = jnp.clip(1.0 + 0.15 * jax.random.normal(keys[1], (D,), jnp.float32), 0.25, 1.75)
    router = gaussian(keys[2], (D, EXPERTS), D ** -0.5, 0.09375)
    expert_gate = gaussian(keys[3], (EXPERTS, D, EH), D ** -0.5, 0.09375, ((0, 32), (2, 4)))
    expert_up = gaussian(keys[4], (EXPERTS, D, EH), D ** -0.5, 0.09375, ((0, 32), (2, 4)))
    expert_down = gaussian(keys[5], (EXPERTS, EH, D), EH ** -0.5, 0.125, ((0, 32), (1, 4)))
    dense_gate = gaussian(keys[6], (D, DH), D ** -0.5, 0.09375, ((0, 32), (1, 4)))
    dense_up = gaussian(keys[7], (D, DH), D ** -0.5, 0.09375, ((0, 32), (1, 4)))
    dense_down_t = gaussian(keys[8], (D, DH), DH ** -0.5, 0.125, ((0, 32), (1, 4)))
    routes_keys = jax.random.split(jax.random.fold_in(keys[9], 1), TOKENS // TOK)
    routes_turns = jax.random.permutation(jax.random.fold_in(keys[9], 3), TOKENS // TOK)
    routes = jax.vmap(lambda own, number: deal_out(jax.random.fold_in(keys[9], 2), own, number, TOK, EXPERTS, 2, CAP, 2))(routes_keys, routes_turns).reshape((TOKENS, 2))
    grad_out = gaussian(keys[10], (TOKENS, D), 1.0, 6.0, ((0, 32),))
    return {"tokens": tokens, "norm_gain": norm_gain, "router": router, "expert_gate": expert_gate, "expert_up": expert_up, "expert_down": expert_down, "dense_gate": dense_gate, "dense_up": dense_up, "dense_down_t": dense_down_t, "routes": routes, "grad_out": grad_out}


NORM_EPS = 1e-05

def silu_parts(pre):
    sigma = jax.nn.sigmoid(pre)
    return (pre * sigma, sigma * (1.0 + pre * (1.0 - sigma)))

def route_slots(block_ids, experts_total):
    flat_ids = block_ids.reshape(-1)
    marks = (flat_ids[:, None] == jnp.arange(experts_total, dtype=jnp.int32)[None, :]).astype(jnp.int32)
    before = jnp.cumsum(marks, axis=0) - marks
    return (flat_ids, lax.optimization_barrier(jnp.sum(before * marks, axis=1)).astype(jnp.int32))

def contract_last(left, right):
    return lax.dot_general(left, right, (((1,), (1,)), ((), ())), preferred_element_type=jnp.float32)

def expert_pass(operands):
    rows, grad_rows, w_gate, w_up, w_down = operands
    gate_pre = jnp.dot(rows, w_gate, preferred_element_type=jnp.float32)
    up_pre = jnp.dot(rows, w_up, preferred_element_type=jnp.float32)
    activated, slope = silu_parts(gate_pre)
    hidden = (activated * up_pre).astype(jnp.bfloat16)
    result = jnp.dot(hidden, w_down, preferred_element_type=jnp.float32)
    hidden_grad = contract_last(grad_rows, w_down)
    gate_grad = (hidden_grad * up_pre * slope).astype(jnp.bfloat16)
    up_grad = (hidden_grad * activated).astype(jnp.bfloat16)
    back = contract_last(gate_grad, w_gate) + contract_last(up_grad, w_up)
    return (result, back)

def reference(tokens, norm_gain, router, expert_gate, expert_up, expert_down, dense_gate, dense_up, dense_down_t, routes, grad_out):
    tokens_wide = tokens.astype(jnp.float32)
    grad_wide = grad_out.astype(jnp.float32)
    row_scale = lax.rsqrt(lax.optimization_barrier(jnp.mean(tokens_wide * tokens_wide, axis=-1, keepdims=True)) + NORM_EPS)
    normed = (tokens_wide * row_scale * norm_gain).astype(jnp.bfloat16)
    logits = jnp.dot(normed, router, preferred_element_type=jnp.float32)
    choose = (routes[:, :, None] == jnp.arange(EXPERTS, dtype=jnp.int32)[None, None, :]).astype(jnp.float32)
    picked = lax.optimization_barrier(jnp.sum(choose * logits[:, None, :], axis=-1))
    gate_first = 1.0 / (1.0 + jnp.exp(picked[:, 1] - picked[:, 0]))
    gate_second = 1.0 - gate_first
    flat_ids, slots = jax.vmap(lambda block: route_slots(block, EXPERTS))(routes.reshape(N_EXPERT, TOK, 2))
    block_index = jnp.arange(N_EXPERT, dtype=jnp.int32)[:, None]
    positions = (block_index * CAP + slots).reshape(-1).astype(jnp.int32)
    flat_ids = flat_ids.reshape(-1).astype(jnp.int32)
    expert_in = jnp.zeros((EXPERTS, EXPERTS * CAP, D), jnp.bfloat16).at[flat_ids, positions].set(jnp.repeat(normed, 2, axis=0))
    expert_grad_in = jnp.zeros((EXPERTS, EXPERTS * CAP, D), jnp.bfloat16).at[flat_ids, positions].set(jnp.repeat(grad_out, 2, axis=0))
    results, backs = lax.map(expert_pass, (expert_in, expert_grad_in, expert_gate, expert_up, expert_down))
    route_out = results[flat_ids, positions].reshape(TOKENS, 2, D)
    route_back = backs[flat_ids, positions].reshape(TOKENS, 2, D)
    dense_gate_pre = jnp.dot(normed, dense_gate, preferred_element_type=jnp.float32)
    dense_up_pre = jnp.dot(normed, dense_up, preferred_element_type=jnp.float32)
    dense_act, dense_slope = silu_parts(dense_gate_pre)
    dense_hidden = (dense_act * dense_up_pre).astype(jnp.bfloat16)
    dense_out = contract_last(dense_hidden, dense_down_t)
    layer_out = (tokens_wide + dense_out + gate_first[:, None] * route_out[:, 0] + gate_second[:, None] * route_out[:, 1]).astype(jnp.bfloat16)
    dense_hidden_grad = jnp.dot(grad_out, dense_down_t, preferred_element_type=jnp.float32)
    dense_gate_grad = (dense_hidden_grad * dense_up_pre * dense_slope).astype(jnp.bfloat16)
    dense_up_grad = (dense_hidden_grad * dense_act).astype(jnp.bfloat16)
    dense_back = contract_last(dense_gate_grad, dense_gate) + contract_last(dense_up_grad, dense_up)
    gate_dot = lax.optimization_barrier(jnp.sum(grad_wide[:, None, :] * route_out, axis=-1))
    logit_grad = gate_first * gate_second * (gate_dot[:, 0] - gate_dot[:, 1])
    router_diff = contract_last((choose[:, 0] - choose[:, 1]).astype(jnp.bfloat16), router)
    normed_grad = dense_back + gate_first[:, None] * route_back[:, 0] + gate_second[:, None] * route_back[:, 1] + logit_grad[:, None] * router_diff
    gained = normed_grad * norm_gain
    grad_in = grad_wide + row_scale * gained - tokens_wide * row_scale ** 3 * lax.optimization_barrier(jnp.mean(tokens_wide * gained, axis=-1, keepdims=True))
    return (layer_out, grad_in.astype(jnp.bfloat16))
```

```python
import itertools

import jax
import jax.numpy as jnp
from jax import lax
from jax.experimental import pallas as pl
from jax.experimental.pallas import tpu as pltpu
from jax.sharding import PartitionSpec as P

NORM_EPS = 1e-05
F32, BF16, I32 = jnp.float32, jnp.bfloat16, jnp.int32
EXPERTS = 32
ROWS = 128
D = 3584
HALF = D // 2
QUARTER = D // 4
HID = 640
PACKED = HALF + QUARTER
LINES = EXPERTS * 8
TILE3 = 384
DENSE_COLS = 3 * TILE3
PIECE = 112
DEVICES = ("expert", "tensor")
VMEM = 56 * 1024 * 1024


def permutation(move):
    sizes = (2, 4, 4, 2, 2)

    def flat(place):
        number = 0
        for at, size in zip(place, sizes):
            number = number * size + at % size
        return number

    return [(flat(p), flat(move(*p))) for p in itertools.product(*map(range, sizes))]


def along_x(step):
    def move(xl, y, z, xh, core):
        x = (xh * 2 + xl + (step if core == 0 else -step)) % 4
        return (x % 2, y, z, x // 2, core)

    return move


SWAP_CORE = permutation(lambda xl, y, z, xh, c: (xl, y, z, xh, 1 - c))
SWAP_XHI = permutation(lambda xl, y, z, xh, c: (xl, y, z, 1 - xh, c))
SWAP_BOTH = permutation(lambda xl, y, z, xh, c: (xl, y, z, 1 - xh, 1 - c))
SWAP_XLO = permutation(lambda xl, y, z, xh, c: (1 - xl, y, z, xh, c))
TO_X = permutation(along_x(1))


def send(value, pairs):
    return lax.ppermute(value, DEVICES, pairs)


def send_y(value, step):
    return send(value, permutation(lambda xl, y, z, xh, c: (xl, y + step, z, xh, c)))


def send_z(value, step):
    return send(value, permutation(lambda xl, y, z, xh, c: (xl, y, z + step, xh, c)))


def dot(left, right, dims=((1,), (0,))):
    return lax.dot_general(left, right, (dims, ((), ())), preferred_element_type=F32)


def dot_last(left, right):
    return dot(left, right, ((1,), (1,)))


def silu_parts(pre):
    sigma = 1.0 / (1.0 + jnp.exp(-pre))
    return (pre * sigma, sigma * (1.0 + pre * (1.0 - sigma)))


def call(kernel, ins, outs, scratch=(), core=None):
    def spec(block, place):
        if block == "any":
            return pl.BlockSpec(memory_space=pl.ANY)
        return pl.BlockSpec(block, place)

    whole = lambda i, c: (0, 0)
    in_specs = []
    for array, block, place in ins:
        if block is None:
            block, place = array.shape, whole
        in_specs.append(spec(block, place))
    return pl.pallas_call(
        kernel,
        grid_spec=pltpu.PrefetchScalarGridSpec(
            num_scalar_prefetch=1,
            grid=(1,),
            in_specs=in_specs,
            out_specs=[pl.BlockSpec(shape, whole) for shape, _ in outs],
            scratch_shapes=list(scratch),
        ),
        out_shape=[jax.ShapeDtypeStruct(shape, dtype) for shape, dtype in outs],
        compiler_params=pltpu.CompilerParams(vmem_limit_bytes=VMEM),
    )(core, *[array for array, _, _ in ins])


MINE_COLS = lambda i, c: (0, c[0])
MINE_ROWS = lambda i, c: (c[0], 0)


def marks_of(routes):
    lanes = lax.broadcasted_iota(I32, (ROWS, EXPERTS), 1)
    return [(routes[:, k : k + 1] == lanes).astype(F32) for k in range(2)]


def place_marks(routes):
    marks = marks_of(routes)
    earlier = (
        lax.broadcasted_iota(I32, (ROWS, ROWS), 1) < lax.broadcasted_iota(I32, (ROWS, ROWS), 0)
    ).astype(BF16)
    before = dot(earlier, (marks[0] + marks[1]).astype(BF16))
    lines = lax.broadcasted_iota(I32, (ROWS, LINES), 1)
    found = []
    for k in range(2):
        slot = jnp.sum(before * marks[k], axis=1, keepdims=True).astype(I32)
        line = routes[:, k : k + 1] * 8 + slot
        first = (slot < 8) & (lines == line)
        low = (slot >= 8) & (lines == line - 8)
        high = (slot >= 8) & (lines == line - 4)
        found.append([m.astype(F32).astype(BF16) for m in (first, low, high)])
    return found


def pack_by_marks(found, rows, out_ref):
    first, low, high = (found[0][i] + found[1][i] for i in range(3))
    down = ((0,), (0,))
    out_ref[:, :HALF] = dot(first, rows, down).astype(BF16)
    out_ref[:, HALF:] = (dot(low, rows[:, :QUARTER], down) + dot(high, rows[:, QUARTER:], down)).astype(BF16)


def grad_dispatch_kernel(core, routes_ref, grad_ref, out_ref):
    pack_by_marks(place_marks(routes_ref[...]), grad_ref[...], out_ref)


def norm_dispatch_kernel(
    core, routes_ref, tokens_ref, part_ref, gain_ref, gain_part_ref, router_ref, out_ref, normed_ref, small_ref
):
    routes = routes_ref[...]
    wide = tokens_ref[...].astype(F32)
    scale = lax.rsqrt(jnp.sum(wide * wide, axis=1, keepdims=True) / D + NORM_EPS)
    normed = (wide * scale * gain_ref[...]).astype(BF16)
    normed_ref[...] = normed
    part = (part_ref[...].astype(F32) * scale * gain_part_ref[...]).astype(BF16)
    pack_by_marks(place_marks(routes), part, out_ref)
    logits = dot(normed, router_ref[...])
    marks = marks_of(routes)
    picked = [jnp.sum(m * logits, axis=1, keepdims=True) for m in marks]
    gate = 1.0 / (1.0 + jnp.exp(picked[1] - picked[0]))
    difference = dot_last((marks[0] - marks[1]).astype(BF16), router_ref[...])
    leaning = jnp.sum(wide * gain_ref[...] * difference, axis=1, keepdims=True)
    lanes = lax.broadcasted_iota(I32, (ROWS, 128), 1)
    small_ref[...] = jnp.where(lanes == 0, scale, jnp.where(lanes == 1, gate, leaning))


def spread_marks():
    q = lax.broadcasted_iota(I32, (ROWS, LINES), 0)
    r = lax.broadcasted_iota(I32, (ROWS, LINES), 1)
    qt = lax.broadcasted_iota(I32, (LINES, ROWS), 1)
    rt = lax.broadcasted_iota(I32, (LINES, ROWS), 0)
    ones = lambda m: m.astype(F32).astype(BF16)
    base, base_t = 2 * q - (q & 3), 2 * qt - (qt & 3)
    return (ones(r == base), ones(r == base + 4)), (ones(rt == base_t), ones(rt == base_t + 4))


def unpack(packed, rows_ref):
    (low, high), _ = spread_marks()
    rows_ref[:LINES, :] = packed[:, :HALF]
    rows_ref[LINES:, :QUARTER] = dot(low, packed[:, HALF:]).astype(BF16)
    rows_ref[LINES:, QUARTER:] = dot(high, packed[:, HALF:]).astype(BF16)


def pack(rows, out_ref):
    _, (low, high) = spread_marks()
    out_ref[:, :HALF] = rows[:LINES].astype(BF16)
    rest = rows[LINES:].astype(BF16)
    out_ref[:, HALF:] = (dot(low, rest[:, :QUARTER]) + dot(high, rest[:, QUARTER:])).astype(BF16)


SLOTS = EXPERTS * 12


def halves(core):
    mine = core[0]
    return [pl.multiple_of(mine * HALF, HALF), pl.multiple_of((1 - mine) * HALF, HALF)]


def begin(copies):
    for copy in copies:
        copy.start()
    return copies


def hidden_grad_kernel(core, mine_ref, other_ref, down_ref, out_ref, down_buf, rows_buf, sems):
    at = halves(core)
    copies = begin(
        [pltpu.make_async_copy(down_ref.at[:, pl.ds(at[h], HALF)], down_buf.at[h], sems.at[h]) for h in range(2)]
    )
    for h, ref in enumerate((mine_ref, other_ref)):
        unpack(ref[...], rows_buf.at[h])
    copies[0].wait()
    part = dot_last(rows_buf[0], down_buf[0])
    copies[1].wait()
    out_ref[...] = part + dot_last(rows_buf[1], down_buf[1])


def expert_forward_kernel(
    core, mine_ref, other_ref, gate_ref, up_ref, down_ref,
    out_mine_ref, out_other_ref, gate_pre_ref, up_pre_ref,
    gate_buf, up_buf, down_buf, rows_buf, sems,
):
    at = halves(core)
    copies = begin(
        [
            pltpu.make_async_copy(src.at[pl.ds(at[h], HALF), :], buf.at[h], sems.at[2 * i + h])
            for i, (src, buf) in enumerate(((gate_ref, gate_buf), (up_ref, up_buf)))
            for h in range(2)
        ]
        + [
            pltpu.make_async_copy(down_ref.at[:, pl.ds(at[h], HALF)], down_buf.at[h], sems.at[4 + h])
            for h in range(2)
        ]
    )
    for h, ref in enumerate((mine_ref, other_ref)):
        unpack(ref[...], rows_buf.at[h])
    copies[0].wait()
    copies[1].wait()
    gate_pre = dot(rows_buf[0], gate_buf[0]) + dot(rows_buf[1], gate_buf[1])
    gate_pre_ref[...] = gate_pre
    copies[2].wait()
    copies[3].wait()
    up_pre = dot(rows_buf[0], up_buf[0]) + dot(rows_buf[1], up_buf[1])
    up_pre_ref[...] = up_pre
    activated, _ = silu_parts(gate_pre)
    hidden = (activated * up_pre).astype(BF16)
    for h, ref in ((1, out_other_ref), (0, out_mine_ref)):
        copies[4 + h].wait()
        pack(dot(hidden, down_buf[h]), ref)


def expert_backward_kernel(
    core, gate_pre_ref, up_pre_ref, hidden_grad_ref, gate_ref, up_ref,
    out_mine_ref, out_other_ref, gate_buf, up_buf, sems,
):
    at = halves(core)
    copies = begin(
        [
            pltpu.make_async_copy(src.at[pl.ds(at[h], HALF), :], buf.at[h], sems.at[2 * h + i])
            for h in (1, 0)
            for i, (src, buf) in enumerate(((gate_ref, gate_buf), (up_ref, up_buf)))
        ]
    )
    activated, slope = silu_parts(gate_pre_ref[...])
    hidden_grad = hidden_grad_ref[...]
    gate_grad = (hidden_grad * up_pre_ref[...] * slope).astype(BF16)
    up_grad = (hidden_grad * activated).astype(BF16)
    for n, (h, ref) in enumerate(((1, out_other_ref), (0, out_mine_ref))):
        copies[2 * n].wait()
        copies[2 * n + 1].wait()
        pack(dot_last(gate_grad, gate_buf[h]) + dot_last(up_grad, up_buf[h]), ref)


def dense_kernel(places, n_pieces, core, rows_ref, own_ref, own_grad_ref, near_m, near_o, near_grad_m, near_grad_o, *refs):
    pieces = refs[:n_pieces]
    out_mine_ref, out_other_ref, weights, rows, grads, sems = refs[n_pieces:]
    at = halves(core)
    near = pl.ds(ROWS, ROWS)
    copies = []

    def copy(source, target):
        copies.append(pltpu.make_async_copy(source, target, sems.at[len(copies)]))
        copies[-1].start()

    copy(own_ref, rows.at[pl.ds(0, ROWS), :])
    copy(own_grad_ref, grads.at[pl.ds(0, ROWS), :])
    for h, (a, b) in enumerate(((near_m, near_grad_m), (near_o, near_grad_o))):
        copy(a, rows.at[near, pl.ds(at[h], HALF)])
        copy(b, grads.at[near, pl.ds(at[h], HALF)])
    for n, (piece, line) in enumerate(places):
        start = pl.multiple_of(rows_ref[n], PIECE)
        copy(pieces[piece].at[pl.ds(line, PIECE), :], weights.at[pl.ds(start, PIECE), :])
    for one in copies:
        one.wait()
    pre = dot(rows[...], weights[:, : 2 * TILE3])
    gate_pre, up_pre = pre[:, :TILE3], pre[:, TILE3:]
    hidden_grad = dot(grads[...], weights[:, 2 * TILE3 :])
    activated, slope = silu_parts(gate_pre)
    hidden = (activated * up_pre).astype(BF16)
    gate_grad = (hidden_grad * up_pre * slope).astype(BF16)
    up_grad = (hidden_grad * activated).astype(BF16)
    for h, ref in ((1, out_other_ref), (0, out_mine_ref)):
        part = pl.ds(at[h], HALF)
        ref[: 2 * ROWS, :] = dot_last(hidden, weights[part, 2 * TILE3 :]).astype(BF16)
        ref[2 * ROWS :, :] = (
            dot_last(gate_grad, weights[part, :TILE3]) + dot_last(up_grad, weights[part, TILE3 : 2 * TILE3])
        ).astype(BF16)


def picked_rows(found, packed):
    first, low, high = found
    rest = packed[:, HALF:]
    return dot(first, packed[:, :HALF]) + jnp.concatenate([dot(low, rest), dot(high, rest)], axis=1)


def combine_forward_kernel(core, routes_ref, back_ref, dense_ref, small_ref, grad_ref, out_ref, dots_ref):
    found = place_marks(routes_ref[...])
    gate = small_ref[:, 1:2]
    one, two = (picked_rows(found[k], back_ref[...]) for k in range(2))
    out_ref[...] = (dense_ref[...].astype(F32) + gate * one + (1.0 - gate) * two).astype(BF16)
    difference = jnp.sum(grad_ref[...].astype(F32) * (one - two), axis=1, keepdims=True)
    dots_ref[...] = jnp.broadcast_to(difference, (ROWS, 128))


def combine_backward_kernel(
    core, routes_ref, back_ref, dense_ref, small_ref, tokens_ref, gain_ref, dots_ref, out_ref, sums_ref
):
    found = place_marks(routes_ref[...])
    gate = small_ref[:, 1:2]
    one, two = (picked_rows(found[k], back_ref[...]) for k in range(2))
    part = dense_ref[...].astype(F32) + gate * one + (1.0 - gate) * two
    out_ref[...] = part.astype(BF16)
    leaning = jnp.sum(tokens_ref[...].astype(F32) * gain_ref[...] * part, axis=1, keepdims=True)
    lanes = lax.broadcasted_iota(I32, (ROWS, 128), 1)
    sums_ref[...] = jnp.where(lanes == 0, dots_ref[...], leaning)


def finish_kernel(
    core, routes_ref, forward_ref, forward_far_ref, back_ref, back_far_ref, sums_a, sums_b, sums_c, sums_d,
    small_ref, tokens_ref, grad_ref, gain_ref, router_ref, layer_ref, grad_in_ref,
):
    tokens = tokens_ref[...].astype(F32)
    layer_ref[...] = (tokens + (forward_ref[...].astype(F32) + forward_far_ref[...].astype(F32))).astype(BF16)
    sums = (sums_a[...] + sums_b[...]) + (sums_c[...] + sums_d[...])
    scale, gate, leaning = small_ref[:, 0:1], small_ref[:, 1:2], small_ref[:, 2:3]
    logit_grad = gate * (1.0 - gate) * sums[:, 0:1]
    mean = (sums[:, 1:2] + logit_grad * leaning) / D
    marks = marks_of(routes_ref[...])
    difference = dot_last((marks[0] - marks[1]).astype(BF16), router_ref[...])
    total = back_ref[...].astype(F32) + back_far_ref[...].astype(F32) + logit_grad * difference
    grad_in = grad_ref[...].astype(F32) + scale * (total * gain_ref[...]) - tokens * (scale * scale * scale * mean)
    grad_in_ref[...] = grad_in.astype(BF16)


def exchange(packed):
    blocks = packed.reshape(EXPERTS, 8, PACKED)
    return lax.all_to_all(blocks, "expert", split_axis=0, concat_axis=0, tiled=True).reshape(LINES, PACKED)


def gather_dense(own, near):
    def around(value, sender):
        return jnp.concatenate([value] + [sender(value, step) for step in (1, 2, 3)], axis=0)

    def across(four, sender):
        after, ahead = sender(four, 1), sender(four, -1)
        cut = 2 * PIECE
        return [four, after, sender(after[:cut], 1), sender(ahead[cut:], -1), ahead]

    own_pieces = across(around(own, send_z), send_y)
    near_pieces = across(around(near, send_y), send_z)
    places = []
    for side in range(2):
        for n, (step, first, count) in enumerate(((0, 0, 4), (1, 0, 4), (2, 0, 2), (2, 2, 2), (3, 0, 4))):
            for k in range(count):
                inner = first + k
                y, z = (step, inner) if side == 0 else (inner, step)
                places.append((5 * side + n, k * PIECE, side, y, z))
    return own_pieces + near_pieces, places


def shards(
    tokens, norm_gain, router, expert_gate, expert_up, expert_down,
    dense_gate, dense_up, dense_down_t, routes, grad_out,
):
    index = lax.axis_index("expert")
    core_index = lax.axis_index("tensor") % 2
    x_lo, y, z = index // 16, (index // 4) % 4, index % 4
    core = core_index.astype(I32).reshape(1)
    gain = norm_gain.reshape(1, D)
    w_gate, w_up, w_down = expert_gate[0], expert_up[0], expert_down[0]

    half = lambda array: (array, (array.shape[0], HALF), MINE_COLS)
    full = lambda array: (array, None, None)
    raw = lambda array: (array, "any", None)

    low = jnp.concatenate([w[:, :TILE3] for w in (dense_gate, dense_up, dense_down_t)], axis=1)
    high = jnp.concatenate(
        [jnp.pad(w[:, TILE3:], ((0, 0), (0, 2 * TILE3 - HID))) for w in (dense_gate, dense_up, dense_down_t)], axis=1
    )
    keeps_low = x_lo == core_index
    own_weights = jnp.where(keeps_low, low, high)
    near_weights = send(jnp.where(keeps_low, high, low), SWAP_XLO)

    (grad_packed,) = call(
        grad_dispatch_kernel, [full(routes), half(grad_out)], [((LINES, PACKED), BF16)], core=core
    )
    grad_mine = exchange(grad_packed)
    norm_packed, normed, small = call(
        norm_dispatch_kernel,
        [full(routes), full(tokens), half(tokens), full(gain), half(gain), full(router)],
        [((LINES, PACKED), BF16), ((ROWS, D), BF16), ((ROWS, 128), F32)],
        core=core,
    )
    norm_mine = exchange(norm_packed)

    cut = lambda array: lax.dynamic_slice_in_dim(array, core_index * HALF, HALF, axis=1)
    near_grad_m = send(cut(grad_out), TO_X)
    near_norm_m = send(cut(normed), TO_X)
    near_grad_o = send(near_grad_m, SWAP_CORE)
    near_norm_o = send(near_norm_m, SWAP_CORE)
    pieces, places = gather_dense(own_weights, near_weights)

    grad_other = send(grad_mine, SWAP_CORE)
    (hidden_grad,) = call(
        hidden_grad_kernel,
        [full(grad_mine), full(grad_other), raw(w_down)],
        [((SLOTS, HID), F32)],
        [pltpu.VMEM((2, HID, HALF), BF16), pltpu.VMEM((2, SLOTS, HALF), BF16), pltpu.SemaphoreType.DMA((2,))],
        core,
    )
    norm_other = send(norm_mine, SWAP_CORE)
    result_mine, result_other, gate_pre, up_pre = call(
        expert_forward_kernel,
        [full(norm_mine), full(norm_other), raw(w_gate), raw(w_up), raw(w_down)],
        [((LINES, PACKED), BF16)] * 2 + [((SLOTS, HID), F32)] * 2,
        [
            pltpu.VMEM((2, HALF, HID), BF16),
            pltpu.VMEM((2, HALF, HID), BF16),
            pltpu.VMEM((2, HID, HALF), BF16),
            pltpu.VMEM((2, SLOTS, HALF), BF16),
            pltpu.SemaphoreType.DMA((6,)),
        ],
        core,
    )

    def joined(mine, other):
        return (mine.astype(F32) + send(other, SWAP_CORE).astype(F32)).astype(BF16)

    back_result = exchange(joined(result_mine, result_other))
    grads_mine, grads_other = call(
        expert_backward_kernel,
        [full(gate_pre), full(up_pre), full(hidden_grad), raw(w_gate), raw(w_up)],
        [((LINES, PACKED), BF16)] * 2,
        [pltpu.VMEM((2, HALF, HID), BF16), pltpu.VMEM((2, HALF, HID), BF16), pltpu.SemaphoreType.DMA((4,))],
        core,
    )
    back_grads = exchange(joined(grads_mine, grads_other))

    starts = jnp.stack(
        [
            ((jnp.where(side == 0, x_lo, 1 - x_lo) * 4 + (y - dy) % 4) * 4 + (z - dz) % 4) * PIECE
            for _, _, side, dy, dz in places
        ]
    ).astype(I32)

    def dense_body(scalars, *refs):
        dense_kernel([p[:2] for p in places], len(pieces), scalars, scalars.at[pl.ds(1, len(places))], *refs)

    dense_mine, dense_other = call(
        dense_body,
        [raw(a) for a in (normed, grad_out, near_norm_m, near_norm_o, near_grad_m, near_grad_o, *pieces)],
        [((4 * ROWS, HALF), BF16)] * 2,
        [
            pltpu.VMEM((D, DENSE_COLS), BF16),
            pltpu.VMEM((2 * ROWS, D), BF16),
            pltpu.VMEM((2 * ROWS, D), BF16),
            pltpu.SemaphoreType.DMA((6 + len(places),)),
        ],
        jnp.concatenate([core, starts]),
    )
    dense_sum = joined(dense_mine, dense_other)
    near_sum = jnp.concatenate([dense_sum[ROWS : 2 * ROWS], dense_sum[3 * ROWS :]], axis=0)
    far_sum = send(near_sum, TO_X).astype(F32)
    dense_forward = dense_sum[:ROWS].astype(F32) + far_sum[:ROWS]
    dense_back = dense_sum[2 * ROWS : 3 * ROWS].astype(F32) + far_sum[ROWS:]

    forward, dots = call(
        combine_forward_kernel,
        [full(routes), full(back_result), full(dense_forward), full(small), half(grad_out)],
        [((ROWS, HALF), BF16), ((ROWS, 128), F32)],
        core=core,
    )
    forward_far = send(forward, SWAP_XHI)
    backward, sums = call(
        combine_backward_kernel,
        [full(routes), full(back_grads), full(dense_back), full(small), half(tokens), half(gain), full(dots)],
        [((ROWS, HALF), BF16), ((ROWS, 128), F32)],
        core=core,
    )
    backward_far = send(backward, SWAP_XHI)
    all_sums = [sums] + [send(sums, pairs) for pairs in (SWAP_XHI, SWAP_CORE, SWAP_BOTH)]
    layer_mine, grad_in_mine = call(
        finish_kernel,
        [full(routes), full(forward), full(forward_far), full(backward), full(backward_far)]
        + [full(s) for s in all_sums]
        + [full(small), half(tokens), half(grad_out), half(gain), (router, (HALF, EXPERTS), MINE_ROWS)],
        [((ROWS, HALF), BF16)] * 2,
        core=core,
    )

    def whole(mine):
        other = send(mine, SWAP_CORE)
        first = core_index == 0
        return jnp.concatenate([jnp.where(first, mine, other), jnp.where(first, other, mine)], axis=1)

    return (whole(layer_mine), whole(grad_in_mine))


def solution(mesh):
    return jax.shard_map(
        shards,
        mesh=mesh,
        in_specs=(
            P("expert", None),
            P(),
            P(),
            P("expert", None, "tensor"),
            P("expert", None, "tensor"),
            P("expert", "tensor", None),
            P("expert", "tensor"),
            P("expert", "tensor"),
            P("expert", "tensor"),
            P("expert", None),
            P("expert", None),
        ),
        out_specs=(P("expert", None), P("expert", None)),
        check_vma=False,
    )
```

```python
import itertools

import jax
import jax.numpy as jnp
from jax import lax
from jax.experimental import pallas as pl
from jax.experimental.pallas import tpu as pltpu
from jax.sharding import PartitionSpec as P

NORM_EPS = 1e-05
F32, BF16, I32 = jnp.float32, jnp.bfloat16, jnp.int32
EXPERTS = 32
ROWS = 128
D = 3584
HALF = D // 2
QUARTER = D // 4
HID = 640
PACKED = HALF + QUARTER
LINES = EXPERTS * 8
SHARE = HID // 2
DENSE_COLS = 1024
PIECE = 112
DEVICES = ("expert", "tensor")


def permutation(move):
    sizes = (2, 4, 4, 2, 2)

    def flat(place):
        number = 0
        for at, size in zip(place, sizes):
            number = number * size + at % size
        return number

    return [(flat(p), flat(move(*p))) for p in itertools.product(*map(range, sizes))]


def along_x(xl, y, z, xh, core):
    x = (xh * 2 + xl + (1 if xl else -1)) % 4
    return (x % 2, y, z, x // 2, core)


SWAP_CORE = permutation(lambda xl, y, z, xh, c: (xl, y, z, xh, 1 - c))
SWAP_XHI = permutation(lambda xl, y, z, xh, c: (xl, y, z, 1 - xh, c))
SWAP_XLO = permutation(lambda xl, y, z, xh, c: (1 - xl, y, z, xh, c))
TO_X = permutation(along_x)


def send(value, pairs):
    return lax.ppermute(value, DEVICES, pairs)


def across(step, first):
    def move(xl, y, z, xh, c):
        return (xl, y, z + step, xh, c) if (c == 0) == first else (xl, y + step, z, xh, c)

    return permutation(move)


def dot(left, right, dims=((1,), (0,))):
    return lax.dot_general(left, right, (dims, ((), ())), preferred_element_type=F32)


def dot_last(left, right):
    return dot(left, right, ((1,), (1,)))


def silu_parts(pre):
    sigma = 1.0 / (1.0 + jnp.exp(-pre))
    return (pre * sigma, sigma * (1.0 + pre * (1.0 - sigma)))


def call(kernel, ins, outs, scratch=(), core=None, takes=3, limit=16):
    place = lambda raw: pl.BlockSpec(memory_space=pl.ANY if raw else pltpu.VMEM)
    return pl.pallas_call(
        kernel,
        in_specs=[pl.BlockSpec(memory_space=pltpu.SMEM)] + [place(raw) for _, raw in ins],
        out_specs=[place(raw == "copied") for _, _, raw in outs],
        scratch_shapes=list(scratch),
        out_shape=[
            pltpu.HBM(shape, dtype) if raw else jax.ShapeDtypeStruct(shape, dtype) for shape, dtype, raw in outs
        ],
        compiler_params=pltpu.CompilerParams(vmem_limit_bytes=limit * 1024 * 1024),
        cost_estimate=pl.CostEstimate(flops=takes * 1_150_000_000, transcendentals=0, bytes_accessed=takes * 3_000_000),
    )(core, *[pltpu.with_memory_space_constraint(array, pltpu.HBM) if raw else array for array, raw in ins])


def begin(sems, *copies):
    begun = [pltpu.make_async_copy(source, target, sems.at[n]) for n, (source, target) in enumerate(copies)]
    for copy in begun:
        copy.start()
    return begun


def halves(core):
    return [pl.multiple_of(core[0] * HALF, HALF), pl.multiple_of((1 - core[0]) * HALF, HALF)]


def routes_of(ref):
    same = lax.broadcasted_iota(I32, (ROWS, ROWS), 0) == lax.broadcasted_iota(I32, (ROWS, ROWS), 1)
    return dot_last(same.astype(F32).astype(BF16), ref[...].astype(F32).astype(BF16)).astype(I32)


def marks_of(routes):
    lanes = lax.broadcasted_iota(I32, (ROWS, EXPERTS), 1)
    return [(routes[:, k : k + 1] == lanes).astype(F32) for k in range(2)]


def place_marks(routes):
    marks = marks_of(routes)
    earlier = (
        lax.broadcasted_iota(I32, (ROWS, ROWS), 1) < lax.broadcasted_iota(I32, (ROWS, ROWS), 0)
    ).astype(BF16)
    before = dot(earlier, (marks[0] + marks[1]).astype(BF16))
    lines = lax.broadcasted_iota(I32, (ROWS, LINES), 1)
    found = []
    for k in range(2):
        slot = jnp.sum(before * marks[k], axis=1, keepdims=True).astype(I32)
        line = routes[:, k : k + 1] * 8 + slot
        first = (slot < 8) & (lines == line)
        low = (slot >= 8) & (lines == line - 8)
        high = (slot >= 8) & (lines == line - 4)
        found.append([m.astype(F32).astype(BF16) for m in (first, low, high)])
    return found


def pack_by_marks(found, rows, out_ref, at):
    first, low, high = (found[0][i] + found[1][i] for i in range(3))
    down = ((0,), (0,))
    rest = dot(low, rows[:, :QUARTER], down) + dot(high, rows[:, QUARTER:], down)
    out_ref[:, at : at + HALF] = dot(first, rows, down).astype(BF16)
    out_ref[:, at + HALF : at + PACKED] = rest.astype(BF16)


def dispatch_kernel(
    core, routes_ref, tokens_ref, gain_ref, router_ref, grad_ref, out_ref, normed_ref, small_ref, share_ref,
):
    routes = routes_of(routes_ref)
    wide = tokens_ref[...].astype(F32)
    scale = lax.rsqrt(jnp.sum(wide * wide, axis=1, keepdims=True) / D + NORM_EPS)
    normed = (wide * scale * gain_ref[...]).astype(BF16)
    normed_ref[...] = normed
    mine = pl.ds(halves(core)[0], HALF)
    part, grad_part = normed_ref[:, mine], grad_ref[:, mine]
    found = place_marks(routes)
    pack_by_marks(found, part, out_ref, 0)
    pack_by_marks(found, grad_part, out_ref, PACKED)
    share_ref[:ROWS, :] = part
    share_ref[ROWS:, :] = grad_part
    logits = dot_last(normed, router_ref[...])
    marks = marks_of(routes)
    picked = [jnp.sum(m * logits, axis=1, keepdims=True) for m in marks]
    gate = 1.0 / (1.0 + jnp.exp(picked[1] - picked[0]))
    difference = dot((marks[0] - marks[1]).astype(BF16), router_ref[...])
    leaning = jnp.sum(wide * gain_ref[...] * difference, axis=1, keepdims=True)
    lanes = lax.broadcasted_iota(I32, (ROWS, 128), 1)
    small_ref[...] = jnp.where(lanes == 0, scale, jnp.where(lanes == 1, gate, leaning))


def spread_marks():
    q = lax.broadcasted_iota(I32, (ROWS, LINES), 0)
    r = lax.broadcasted_iota(I32, (ROWS, LINES), 1)
    qt = lax.broadcasted_iota(I32, (LINES, ROWS), 1)
    rt = lax.broadcasted_iota(I32, (LINES, ROWS), 0)
    ones = lambda m: m.astype(F32).astype(BF16)
    base, base_t = 2 * q - (q & 3), 2 * qt - (qt & 3)
    return (ones(r == base), ones(r == base + 4)), (ones(rt == base_t), ones(rt == base_t + 4))


def unpack(packed, rows_ref):
    (low, high), _ = spread_marks()
    rows_ref[:LINES, :] = packed[:, :HALF]
    rows_ref[LINES:, :QUARTER] = dot(low, packed[:, HALF:]).astype(BF16)
    rows_ref[LINES:, QUARTER:] = dot(high, packed[:, HALF:]).astype(BF16)


def pack(rows, out_ref):
    _, (low, high) = spread_marks()
    out_ref[:, :HALF] = rows[:LINES].astype(BF16)
    rest = rows[LINES:].astype(BF16)
    out_ref[:, HALF:] = (dot(low, rest[:, :QUARTER]) + dot(high, rest[:, QUARTER:])).astype(BF16)


SLOTS = EXPERTS * 12


def expert_forward_kernel(
    core, mine_ref, other_ref, gate_hbm, up_hbm, down_hbm,
    out_mine_ref, out_other_ref, gate_pre_hbm, up_pre_hbm,
    gate_ref, up_ref, down_ref, gate_pre_ref, up_pre_ref, rows, sems,
):
    at = halves(core)
    parts = [pl.ds(at[h], HALF) for h in range(2)]
    gate = begin(sems.at[pl.ds(0, 2)], *[(gate_hbm.at[p, :], gate_ref.at[p, :]) for p in parts])
    for h, ref in enumerate((mine_ref, other_ref)):
        unpack(ref[:, :PACKED], rows.at[h])
    up = begin(sems.at[pl.ds(2, 2)], *[(up_hbm.at[p, :], up_ref.at[p, :]) for p in parts])
    gate[0].wait()
    product = dot(rows[0], gate_ref[parts[0], :])
    gate[1].wait()
    gate_pre_ref[...] = product + dot(rows[1], gate_ref[parts[1], :])
    down = begin(sems.at[pl.ds(4, 2)], *[(down_hbm.at[:, p], down_ref.at[:, p]) for p in reversed(parts)])
    up[0].wait()
    product = dot(rows[0], up_ref[parts[0], :])
    up[1].wait()
    up_pre_ref[...] = product + dot(rows[1], up_ref[parts[1], :])
    written = begin(sems.at[pl.ds(6, 2)], (gate_pre_ref, gate_pre_hbm), (up_pre_ref, up_pre_hbm))
    activated, _ = silu_parts(gate_pre_ref[...])
    hidden = (activated * up_pre_ref[...]).astype(BF16)
    for n, (h, ref) in enumerate(((1, out_other_ref), (0, out_mine_ref))):
        down[n].wait()
        pack(dot(hidden, down_ref[:, parts[h]]), ref)
    for copy in written:
        copy.wait()


def expert_backward_kernel(
    core, mine_hbm, other_hbm, gate_pre_hbm, up_pre_hbm, gate_hbm, up_hbm, down_hbm, after_ref,
    out_mine_ref, out_other_ref,
    gate_ref, up_ref, down_ref, gate_pre_ref, up_pre_ref, rows, arrived, sems,
):
    del after_ref
    at = halves(core)
    parts = [pl.ds(at[h], HALF) for h in range(2)]
    last = pl.ds(PACKED, PACKED)
    incoming = begin(
        sems.at[pl.ds(0, 4)],
        *[
            copy
            for h, ref in enumerate((mine_hbm, other_hbm))
            for copy in ((ref.at[:, last], arrived.at[h]), (down_hbm.at[:, parts[h]], down_ref.at[:, parts[h]]))
        ],
    )
    hidden_grad = 0.0
    for h in range(2):
        incoming[2 * h].wait()
        unpack(arrived[h], rows.at[h])
        incoming[2 * h + 1].wait()
        if h == 0:
            pre = begin(sems.at[pl.ds(4, 2)], (gate_pre_hbm, gate_pre_ref), (up_pre_hbm, up_pre_ref))
            weights = begin(
                sems.at[pl.ds(6, 4)],
                *[
                    copy
                    for p in reversed(parts)
                    for copy in ((gate_hbm.at[p, :], gate_ref.at[p, :]), (up_hbm.at[p, :], up_ref.at[p, :]))
                ],
            )
        hidden_grad = hidden_grad + dot_last(rows[h], down_ref[:, parts[h]])
    for copy in pre:
        copy.wait()
    activated, slope = silu_parts(gate_pre_ref[...])
    gate_grad = (hidden_grad * up_pre_ref[...] * slope).astype(BF16)
    up_grad = (hidden_grad * activated).astype(BF16)
    for n, (h, ref) in enumerate(((1, out_other_ref), (0, out_mine_ref))):
        weights[2 * n].wait()
        product = dot_last(gate_grad, gate_ref[parts[h], :])
        weights[2 * n + 1].wait()
        pack(product + dot_last(up_grad, up_ref[parts[h], :]), ref)


def split_weights_kernel(low, gate_ref, up_ref, down_ref, after_ref, own_ref, near_ref):
    rest = jnp.zeros((PIECE, DENSE_COLS - 3 * SHARE), F32)
    wide = [ref[...].astype(F32) for ref in (gate_ref, up_ref, down_ref)]
    first = jnp.concatenate([w[:, :SHARE] for w in wide] + [rest], axis=1).astype(BF16)
    second = jnp.concatenate([w[:, SHARE:] for w in wide] + [rest], axis=1).astype(BF16)

    @pl.when(low[0] == 0)
    def _():
        own_ref[...] = first
        near_ref[...] = second

    @pl.when(low[0] != 0)
    def _():
        own_ref[...] = second
        near_ref[...] = first


def dense_kernel(core, *refs):
    own_ref, own_grad_ref, near_m, near_o, *pieces = refs[: 4 + PIECES]
    _, out_mine_ref, out_other_ref, weights, rows, grads, sems = refs[4 + PIECES :]
    at = halves(core)
    near = pl.ds(ROWS, ROWS)
    copies = []

    def copy(source, target):
        copies.append(pltpu.make_async_copy(source, target, sems.at[len(copies)]))
        copies[-1].start()

    copy(own_ref, rows.at[pl.ds(0, ROWS), :])
    copy(own_grad_ref, grads.at[pl.ds(0, ROWS), :])
    for h, ref in enumerate((near_m, near_o)):
        copy(ref.at[pl.ds(0, ROWS), :], rows.at[near, pl.ds(at[h], HALF)])
        copy(ref.at[near, :], grads.at[near, pl.ds(at[h], HALF)])
    for n, (piece, line, *_) in enumerate(PLACES):
        start = pl.multiple_of(core[1 + n], PIECE)
        copy(pieces[piece].at[pl.ds(line, PIECE), :], weights.at[pl.ds(start, PIECE), :])
    for one in copies:
        one.wait()
    pre = dot(rows[...], weights[:, : 2 * SHARE])
    gate_pre, up_pre = pre[:, :SHARE], pre[:, SHARE:]
    hidden_grad = dot(grads[...], weights[:, 512:])[:, 2 * SHARE - 512 : 3 * SHARE - 512]
    activated, slope = silu_parts(gate_pre)
    zeros = lambda n: jnp.zeros((2 * ROWS, n), F32)
    hidden = jnp.concatenate([zeros(2 * SHARE - 512), activated * up_pre, zeros(DENSE_COLS - 3 * SHARE)], axis=1)
    hidden = hidden.astype(BF16)
    pre_grad = jnp.concatenate([hidden_grad * up_pre * slope, hidden_grad * activated], axis=1).astype(BF16)
    for h, ref in ((1, out_other_ref), (0, out_mine_ref)):
        part = pl.ds(at[h], HALF)
        forward = dot_last(hidden, weights[part, 512:]).astype(BF16)
        ref[:ROWS, :] = forward[:ROWS]
        ref[2 * ROWS : 3 * ROWS, :] = forward[ROWS:]
        backward = dot_last(pre_grad, weights[part, : 2 * SHARE]).astype(BF16)
        ref[ROWS : 2 * ROWS, :] = backward[:ROWS]
        ref[3 * ROWS :, :] = backward[ROWS:]


def picked_rows(found, packed):
    first, low, high = found
    rest = packed[:, HALF:]
    return dot(first, packed[:, :HALF]) + jnp.concatenate([dot(low, rest), dot(high, rest)], axis=1)


def thirds(column):
    lanes = lax.broadcasted_iota(I32, (ROWS, 128), 1)
    high = column.astype(BF16).astype(F32)
    middle = (column - high).astype(BF16).astype(F32)
    low = column - high - middle
    return jnp.where(lanes == 0, high, jnp.where(lanes == 1, middle, jnp.where(lanes == 2, low, 0.0))).astype(BF16)


def total(columns):
    return jnp.sum(columns.astype(F32), axis=1, keepdims=True)


def combine(core, routes_ref, back_ref, dense_refs, small_hbm, features_hbm, bufs, sems, first):
    dense, small, features = bufs
    rows = pl.ds(first, ROWS)
    mine = pl.ds(halves(core)[0], HALF)
    sources = [dense_refs[0].at[rows, :], dense_refs[1].at[rows, :], dense_refs[2]]
    copies = begin(
        sems,
        *[(source, dense.at[n]) for n, source in enumerate(sources)],
        (small_hbm, small),
        (features_hbm.at[:, mine], features),
    )
    found = place_marks(routes_of(routes_ref))
    one, two = (picked_rows(found[k], back_ref[...]) for k in range(2))
    for copy in copies:
        copy.wait()
    gate = small[:, 1:2]
    part = dense[0].astype(F32) + dense[1].astype(F32) + dense[2].astype(F32)
    return one, two, part + gate * one + (1.0 - gate) * two


def combine_forward_kernel(
    core, routes_ref, back_ref, dense_a, dense_b, dense_c, small_ref, grad_ref, out_ref, dense, small, grad, sems
):
    one, two, part = combine(
        core, routes_ref, back_ref, (dense_a, dense_b, dense_c), small_ref, grad_ref, (dense, small, grad), sems, 0
    )
    out_ref[:, :HALF] = part.astype(BF16)
    out_ref[:, HALF:] = thirds(jnp.sum(grad[...].astype(F32) * (one - two), axis=1, keepdims=True))


def combine_backward_kernel(
    core, routes_ref, back_ref, dense_a, dense_b, dense_c, small_ref, tokens_ref, gain_ref, out_ref,
    dense, small, tokens, sems,
):
    _, _, part = combine(
        core, routes_ref, back_ref, (dense_a, dense_b, dense_c), small_ref, tokens_ref, (dense, small, tokens), sems, ROWS
    )
    out_ref[:, :HALF] = part.astype(BF16)
    weighted = tokens[...].astype(F32) * gain_ref[:, pl.ds(halves(core)[0], HALF)] * part
    out_ref[:, HALF:] = thirds(jnp.sum(weighted, axis=1, keepdims=True))


def add_far_kernel(core, forward_ref, forward_far_ref, back_ref, back_far_ref, tokens_ref, out_ref):
    layer = tokens_ref[:, pl.ds(halves(core)[0], HALF)].astype(F32) + (
        forward_ref[:, :HALF].astype(F32) + forward_far_ref[:, :HALF].astype(F32)
    )
    out_ref[:ROWS, :HALF] = layer.astype(BF16)
    out_ref[ROWS:, :HALF] = (back_ref[:, :HALF].astype(F32) + back_far_ref[:, :HALF].astype(F32)).astype(BF16)
    out_ref[:ROWS, HALF:] = thirds(total(forward_ref[:, HALF:]) + total(forward_far_ref[:, HALF:]))
    out_ref[ROWS:, HALF:] = thirds(total(back_ref[:, HALF:]) + total(back_far_ref[:, HALF:]))


def finish_kernel(
    core, routes_ref, mine_ref, other_ref, small_ref, tokens_ref, grad_ref, gain_ref, router_ref,
    layer_ref, grad_in_ref,
):
    scale, gate, leaning = small_ref[:, 0:1], small_ref[:, 1:2], small_ref[:, 2:3]
    dots, sums = (
        total(mine_ref[rows, HALF:]) + total(other_ref[rows, HALF:]) for rows in (slice(0, ROWS), slice(ROWS, None))
    )
    logit_grad = gate * (1.0 - gate) * dots
    mean = scale * scale * scale * ((sums + logit_grad * leaning) / D)
    marks = marks_of(routes_of(routes_ref))
    difference = (marks[0] - marks[1]).astype(BF16)
    at = halves(core)
    for h, ref in enumerate((mine_ref, other_ref)):
        part = pl.ds(at[h], HALF)
        layer_ref[:, part] = ref[:ROWS, :HALF]
        grown = ref[ROWS:, :HALF].astype(F32) + logit_grad * dot(difference, router_ref[:, part])
        moved = scale * (grown * gain_ref[:, part]) - tokens_ref[:, part].astype(F32) * mean
        grad_in_ref[:, part] = (grad_ref[:, part].astype(F32) + moved).astype(BF16)


def exchange(packed):
    blocks = packed.reshape(EXPERTS, 8, packed.shape[1])
    return lax.all_to_all(blocks, "expert", split_axis=0, concat_axis=0, tiled=True).reshape(packed.shape)


PIECES = 8


PLACES = [
    (n, (2 * k + side) * PIECE, side, 2 * (n % 2) + k, n // 2)
    for n in range(PIECES)
    for k in range(2)
    for side in range(2)
]


def shards(
    tokens, norm_gain, router, expert_gate, expert_up, expert_down,
    dense_gate, dense_up, dense_down_t, routes, grad_out,
):
    index = lax.axis_index("expert")
    core_index = lax.axis_index("tensor") % 2
    x_lo, y, z = index // 16, (index // 4) % 4, index % 4
    core = core_index.astype(I32).reshape(1)
    gain = norm_gain.reshape(1, D)
    w_gate, w_up, w_down = expert_gate[0], expert_up[0], expert_down[0]

    full = lambda array: (array, False)
    raw = lambda array: (array, True)
    hbm = lambda *shape: (shape, BF16, True)
    kept = lambda *shape: (shape, BF16, False)

    routes = routes.T
    router = router.T

    packed, normed, small, share = call(
        dispatch_kernel,
        [full(routes), full(tokens), full(gain), full(router), full(grad_out)],
        [hbm(LINES, 2 * PACKED), hbm(ROWS, D), ((ROWS, 128), F32, True), hbm(2 * ROWS, HALF)],
        core=core,
        takes=7,
    )

    own_weights, near_weights = call(
        split_weights_kernel,
        [full(dense_gate), full(dense_up), full(dense_down_t), raw(routes)],
        [kept(PIECE, DENSE_COLS)] * 2,
        core=x_lo.astype(I32).reshape(1),
    )
    pair = jnp.concatenate([own_weights, send(near_weights, SWAP_XLO)], axis=0)
    packed, pair = lax.optimization_barrier((packed, pair))
    arrived, near_mine, *around = lax.optimization_barrier(
        (exchange(packed), send(share, TO_X), *[send(pair, across(n, True)) for n in (1, 2, 3)])
    )
    low, high = jnp.concatenate([pair, around[0]], axis=0), jnp.concatenate(around[1:], axis=0)
    low_after, high_ahead = send(low, across(1, False)), send(high, across(3, False))
    high_after, low_ahead = send(high, across(1, False)), send(low, across(3, False))

    near_other = send(near_mine, SWAP_CORE)

    arrived_other = send(arrived, SWAP_CORE)
    weights = [raw(w_gate), raw(w_up), raw(w_down)]
    buffers = [pltpu.VMEM((D, HID), BF16), pltpu.VMEM((D, HID), BF16), pltpu.VMEM((HID, D), BF16)]
    buffers += [pltpu.VMEM((SLOTS, HID), F32)] * 2 + [pltpu.VMEM((2, SLOTS, HALF), BF16)]
    result_mine, result_other, gate_pre, up_pre = call(
        expert_forward_kernel,
        [full(arrived), full(arrived_other), *weights],
        [hbm(LINES, PACKED), kept(LINES, PACKED)] + [((SLOTS, HID), F32, "copied")] * 2,
        buffers + [pltpu.SemaphoreType.DMA((8,))],
        core,
        takes=14,
        limit=40,
    )
    result_mine, result_other, low_after, high_ahead, near_other = lax.optimization_barrier(
        (result_mine, result_other, low_after, high_ahead, near_other)
    )
    low_far, high_far = send(low_after, across(1, False)), send(high_ahead, across(3, False))

    def joined(mine, other):
        return (mine.astype(F32) + send(other, SWAP_CORE).astype(F32)).astype(BF16)

    result = joined(result_mine, result_other)
    back_result = exchange(result)
    grads_mine, grads_other = call(
        expert_backward_kernel,
        [raw(arrived), raw(arrived_other), raw(gate_pre), raw(up_pre), *weights, raw(result)],
        [hbm(LINES, PACKED), kept(LINES, PACKED)],
        buffers + [pltpu.VMEM((2, LINES, PACKED), BF16), pltpu.SemaphoreType.DMA((10,))],
        core,
        takes=14,
        limit=40,
    )

    def start_of(side, first, second):
        dy, dz = jnp.where(core_index == 0, second, first), jnp.where(core_index == 0, first, second)
        return (((x_lo + side) % 2 * 4 + (y - dy) % 4) * 4 + (z - dz) % 4) * PIECE

    table = jnp.array([place[2:] for place in PLACES], I32)
    starts = start_of(table[:, 0], table[:, 1], table[:, 2]).astype(I32)

    pieces = [low, high, low_after, high_after, low_far, high_far, low_ahead, high_ahead]
    dense_mine, dense_other = call(
        dense_kernel,
        [raw(a) for a in (normed, grad_out, near_mine, near_other, *pieces, grads_other)],
        [hbm(4 * ROWS, HALF), kept(4 * ROWS, HALF)],
        [
            pltpu.VMEM((D, DENSE_COLS), BF16),
            pltpu.VMEM((2 * ROWS, D), BF16),
            pltpu.VMEM((2 * ROWS, D), BF16),
            pltpu.SemaphoreType.DMA((6 + len(PLACES),)),
        ],
        jnp.concatenate([core, starts]),
        takes=12,
        limit=28,
    )
    dense_other, grads_other, back_result = lax.optimization_barrier((dense_other, grads_other, back_result))
    dense_far = send(dense_other, SWAP_CORE)
    near_sums = [
        (dense_mine[a : a + ROWS].astype(F32) + dense_far[a : a + ROWS].astype(F32)).astype(BF16)
        for a in (2 * ROWS, 3 * ROWS)
    ]
    grads, *near_sums = lax.optimization_barrier((joined(grads_mine, grads_other), *near_sums))
    back_grads = exchange(grads)

    def dense_part(n):
        return [raw(dense_mine), raw(dense_far), raw(send(near_sums[n], TO_X))]

    row_buffers = [pltpu.VMEM((3, ROWS, HALF), BF16), pltpu.VMEM((ROWS, 128), F32), pltpu.VMEM((ROWS, HALF), BF16)]
    row_buffers += [pltpu.SemaphoreType.DMA((5,))]
    (forward,) = call(
        combine_forward_kernel,
        [full(routes), full(back_result), *dense_part(0), raw(small), raw(grad_out)],
        [kept(ROWS, HALF + 128)],
        row_buffers,
        core=core,
    )
    forward, back_grads = lax.optimization_barrier((forward, back_grads))
    forward_far = send(forward, SWAP_XHI)
    (backward,) = call(
        combine_backward_kernel,
        [full(routes), full(back_grads), *dense_part(1), raw(small), raw(tokens), full(gain)],
        [kept(ROWS, HALF + 128)],
        row_buffers,
        core=core,
    )
    backward, forward_far = lax.optimization_barrier((backward, forward_far))
    backward_far = send(backward, SWAP_XHI)
    (mine,) = call(
        add_far_kernel,
        [full(forward), full(forward_far), full(backward), full(backward_far), full(tokens)],
        [kept(2 * ROWS, HALF + 128)],
        core=core,
    )
    return tuple(
        call(
            finish_kernel,
            [full(routes), full(mine), full(send(mine, SWAP_CORE)), full(small)]
            + [full(tokens), full(grad_out), full(gain), full(router)],
            [kept(ROWS, D)] * 2,
            core=core,
        )
    )


def solution(mesh):
    return jax.shard_map(
        shards,
        mesh=mesh,
        in_specs=(
            P("expert", None),
            P(),
            P(),
            P("expert", None, "tensor"),
            P("expert", None, "tensor"),
            P("expert", "tensor", None),
            P("expert", "tensor"),
            P("expert", "tensor"),
            P("expert", "tensor"),
            P("expert", None),
            P("expert", None),
        ),
        out_specs=(P("expert", None), P("expert", None)),
        check_vma=False,
    )
```

```python
import itertools

import jax
import jax.numpy as jnp
from jax import lax
from jax.experimental import pallas as pl
from jax.experimental.pallas import tpu as pltpu
from jax.sharding import PartitionSpec as P

NORM_EPS = 1e-05
F32, BF16, I32 = jnp.float32, jnp.bfloat16, jnp.int32
EXPERTS = 32
ROWS = 128
D = 3584
HALF = D // 2
QUARTER = D // 4
HID = 640
PACKED = HALF + QUARTER
LINES = EXPERTS * 8
SHARE = HID // 2
DENSE_COLS = 1024
PIECE = 112
DEVICES = ("expert", "tensor")


def permutation(move):
    sizes = (2, 4, 4, 2, 2)

    def flat(place):
        number = 0
        for at, size in zip(place, sizes):
            number = number * size + at % size
        return number

    return [(flat(p), flat(move(*p))) for p in itertools.product(*map(range, sizes))]


def along_x(xl, y, z, xh, core):
    x = (xh * 2 + xl + (1 if xl else -1)) % 4
    return (x % 2, y, z, x // 2, core)


SWAP_CORE = permutation(lambda xl, y, z, xh, c: (xl, y, z, xh, 1 - c))
SWAP_XHI = permutation(lambda xl, y, z, xh, c: (xl, y, z, 1 - xh, c))
SWAP_XLO = permutation(lambda xl, y, z, xh, c: (1 - xl, y, z, xh, c))
TO_X = permutation(along_x)


def send(value, pairs):
    return lax.ppermute(value, DEVICES, pairs)


def across(step, first):
    def move(xl, y, z, xh, c):
        return (xl, y, z + step, xh, c) if (c == 0) == first else (xl, y + step, z, xh, c)

    return permutation(move)


def dot(left, right, dims=((1,), (0,))):
    return lax.dot_general(left, right, (dims, ((), ())), preferred_element_type=F32)


def dot_last(left, right):
    return dot(left, right, ((1,), (1,)))


def silu_parts(pre):
    sigma = 1.0 / (1.0 + jnp.exp(-pre))
    return (pre * sigma, sigma * (1.0 + pre * (1.0 - sigma)))


def call(kernel, ins, outs, scratch=(), core=None, takes=3, limit=16):
    place = lambda raw: pl.BlockSpec(memory_space=pl.ANY if raw else pltpu.VMEM)
    return pl.pallas_call(
        kernel,
        in_specs=[pl.BlockSpec(memory_space=pltpu.SMEM)] + [place(raw) for _, raw in ins],
        out_specs=[place(raw == "copied") for _, _, raw in outs],
        scratch_shapes=list(scratch),
        out_shape=[
            pltpu.HBM(shape, dtype) if raw else jax.ShapeDtypeStruct(shape, dtype) for shape, dtype, raw in outs
        ],
        compiler_params=pltpu.CompilerParams(vmem_limit_bytes=limit * 1024 * 1024),
        cost_estimate=pl.CostEstimate(flops=takes * 1_150_000_000, transcendentals=0, bytes_accessed=takes * 3_000_000),
    )(core, *[pltpu.with_memory_space_constraint(array, pltpu.HBM) if raw else array for array, raw in ins])


def begin(sems, *copies):
    begun = [pltpu.make_async_copy(source, target, sems.at[n]) for n, (source, target) in enumerate(copies)]
    for copy in begun:
        copy.start()
    return begun


def halves(core):
    return [pl.multiple_of(core[0] * HALF, HALF), pl.multiple_of((1 - core[0]) * HALF, HALF)]


def routes_of(ref):
    same = lax.broadcasted_iota(I32, (ROWS, ROWS), 0) == lax.broadcasted_iota(I32, (ROWS, ROWS), 1)
    return dot_last(same.astype(F32).astype(BF16), ref[...].astype(F32).astype(BF16)).astype(I32)


def marks_of(routes):
    lanes = lax.broadcasted_iota(I32, (ROWS, EXPERTS), 1)
    return [(routes[:, k : k + 1] == lanes).astype(F32) for k in range(2)]


def place_marks(routes):
    marks = marks_of(routes)
    earlier = (
        lax.broadcasted_iota(I32, (ROWS, ROWS), 1) < lax.broadcasted_iota(I32, (ROWS, ROWS), 0)
    ).astype(BF16)
    before = dot(earlier, (marks[0] + marks[1]).astype(BF16))
    lines = lax.broadcasted_iota(I32, (ROWS, LINES), 1)
    found = []
    for k in range(2):
        slot = jnp.sum(before * marks[k], axis=1, keepdims=True).astype(I32)
        line = routes[:, k : k + 1] * 8 + slot
        first = (slot < 8) & (lines == line)
        low = (slot >= 8) & (lines == line - 8)
        high = (slot >= 8) & (lines == line - 4)
        found.append([m.astype(F32).astype(BF16) for m in (first, low, high)])
    return found


def pack_by_marks(found, rows, out_ref, at):
    first, low, high = (found[0][i] + found[1][i] for i in range(3))
    down = ((0,), (0,))
    rest = dot(low, rows[:, :QUARTER], down) + dot(high, rows[:, QUARTER:], down)
    out_ref[:, at : at + HALF] = dot(first, rows, down).astype(BF16)
    out_ref[:, at + HALF : at + PACKED] = rest.astype(BF16)


def dispatch_kernel(
    core, routes_ref, tokens_ref, gain_ref, grad_ref, out_ref, normed_ref, scale_ref, share_ref,
):
    routes = routes_of(routes_ref)
    wide = tokens_ref[...].astype(F32)
    scale = lax.rsqrt(jnp.sum(wide * wide, axis=1, keepdims=True) / D + NORM_EPS)
    normed = (wide * scale * gain_ref[...]).astype(BF16)
    normed_ref[...] = normed
    mine = pl.ds(halves(core)[0], HALF)
    part, grad_part = normed_ref[:, mine], grad_ref[:, mine]
    found = place_marks(routes)
    pack_by_marks(found, part, out_ref, 0)
    pack_by_marks(found, grad_part, out_ref, PACKED)
    share_ref[:ROWS, :] = part
    share_ref[ROWS:, :] = grad_part
    scale_ref[...] = jnp.broadcast_to(scale, (ROWS, 128))


def gates_kernel(core, routes_ref, tokens_ref, gain_ref, router_ref, normed_ref, scale_ref, small_ref):
    wide, normed, scale = tokens_ref[...].astype(F32), normed_ref[...], scale_ref[:, 0:1]
    logits = dot_last(normed, router_ref[...])
    marks = marks_of(routes_of(routes_ref))
    picked = [jnp.sum(m * logits, axis=1, keepdims=True) for m in marks]
    gate = 1.0 / (1.0 + jnp.exp(picked[1] - picked[0]))
    difference = dot((marks[0] - marks[1]).astype(BF16), router_ref[...])
    leaning = jnp.sum(wide * gain_ref[...] * difference, axis=1, keepdims=True)
    lanes = lax.broadcasted_iota(I32, (ROWS, 128), 1)
    small_ref[...] = jnp.where(lanes == 0, scale, jnp.where(lanes == 1, gate, leaning))


def spread_marks():
    q = lax.broadcasted_iota(I32, (ROWS, LINES), 0)
    r = lax.broadcasted_iota(I32, (ROWS, LINES), 1)
    qt = lax.broadcasted_iota(I32, (LINES, ROWS), 1)
    rt = lax.broadcasted_iota(I32, (LINES, ROWS), 0)
    ones = lambda m: m.astype(F32).astype(BF16)
    base, base_t = 2 * q - (q & 3), 2 * qt - (qt & 3)
    return (ones(r == base), ones(r == base + 4)), (ones(rt == base_t), ones(rt == base_t + 4))


def unpack(packed, rows_ref):
    (low, high), _ = spread_marks()
    rows_ref[:LINES, :] = packed[:, :HALF]
    rows_ref[LINES:, :QUARTER] = dot(low, packed[:, HALF:]).astype(BF16)
    rows_ref[LINES:, QUARTER:] = dot(high, packed[:, HALF:]).astype(BF16)


def pack(rows, out_ref):
    _, (low, high) = spread_marks()
    out_ref[:, :HALF] = rows[:LINES].astype(BF16)
    rest = rows[LINES:].astype(BF16)
    out_ref[:, HALF:] = (dot(low, rest[:, :QUARTER]) + dot(high, rest[:, QUARTER:])).astype(BF16)


SLOTS = EXPERTS * 12


def expert_forward_kernel(
    core, mine_ref, other_ref, gate_hbm, up_hbm, down_hbm,
    out_mine_ref, out_other_ref, gate_pre_hbm, up_pre_hbm,
    gate_ref, up_ref, down_ref, gate_pre_ref, up_pre_ref, rows, sems,
):
    at = halves(core)
    parts = [pl.ds(at[h], HALF) for h in range(2)]
    gate = begin(sems.at[pl.ds(0, 2)], *[(gate_hbm.at[p, :], gate_ref.at[p, :]) for p in parts])
    for h, ref in enumerate((mine_ref, other_ref)):
        unpack(ref[:, :PACKED], rows.at[h])
    up = begin(sems.at[pl.ds(2, 2)], *[(up_hbm.at[p, :], up_ref.at[p, :]) for p in parts])
    gate[0].wait()
    product = dot(rows[0], gate_ref[parts[0], :])
    gate[1].wait()
    gate_pre_ref[...] = product + dot(rows[1], gate_ref[parts[1], :])
    down = begin(sems.at[pl.ds(4, 2)], *[(down_hbm.at[:, p], down_ref.at[:, p]) for p in reversed(parts)])
    up[0].wait()
    product = dot(rows[0], up_ref[parts[0], :])
    up[1].wait()
    up_pre_ref[...] = product + dot(rows[1], up_ref[parts[1], :])
    written = begin(sems.at[pl.ds(6, 2)], (gate_pre_ref, gate_pre_hbm), (up_pre_ref, up_pre_hbm))
    activated, _ = silu_parts(gate_pre_ref[...])
    hidden = (activated * up_pre_ref[...]).astype(BF16)
    for n, (h, ref) in enumerate(((1, out_other_ref), (0, out_mine_ref))):
        down[n].wait()
        pack(dot(hidden, down_ref[:, parts[h]]), ref)
    for copy in written:
        copy.wait()


def expert_backward_kernel(
    core, mine_hbm, other_hbm, gate_pre_hbm, up_pre_hbm, gate_hbm, up_hbm, down_hbm, after_ref,
    out_mine_ref, out_other_ref,
    gate_ref, up_ref, down_ref, gate_pre_ref, up_pre_ref, rows, arrived, sems,
):
    del after_ref
    at = halves(core)
    parts = [pl.ds(at[h], HALF) for h in range(2)]
    last = pl.ds(PACKED, PACKED)
    incoming = begin(
        sems.at[pl.ds(0, 4)],
        *[
            copy
            for h, ref in enumerate((mine_hbm, other_hbm))
            for copy in ((ref.at[:, last], arrived.at[h]), (down_hbm.at[:, parts[h]], down_ref.at[:, parts[h]]))
        ],
    )
    hidden_grad = 0.0
    for h in range(2):
        incoming[2 * h].wait()
        unpack(arrived[h], rows.at[h])
        incoming[2 * h + 1].wait()
        if h == 0:
            pre = begin(sems.at[pl.ds(4, 2)], (gate_pre_hbm, gate_pre_ref), (up_pre_hbm, up_pre_ref))
            weights = begin(
                sems.at[pl.ds(6, 4)],
                *[
                    copy
                    for p in reversed(parts)
                    for copy in ((gate_hbm.at[p, :], gate_ref.at[p, :]), (up_hbm.at[p, :], up_ref.at[p, :]))
                ],
            )
        hidden_grad = hidden_grad + dot_last(rows[h], down_ref[:, parts[h]])
    for copy in pre:
        copy.wait()
    activated, slope = silu_parts(gate_pre_ref[...])
    gate_grad = (hidden_grad * up_pre_ref[...] * slope).astype(BF16)
    up_grad = (hidden_grad * activated).astype(BF16)
    for n, (h, ref) in enumerate(((1, out_other_ref), (0, out_mine_ref))):
        weights[2 * n].wait()
        product = dot_last(gate_grad, gate_ref[parts[h], :])
        weights[2 * n + 1].wait()
        pack(product + dot_last(up_grad, up_ref[parts[h], :]), ref)


def split_weights_kernel(low, gate_hbm, up_hbm, down_hbm, own_ref, near_ref, gate_ref, up_ref, down_ref, sems):
    for copy in begin(sems, (gate_hbm, gate_ref), (up_hbm, up_ref), (down_hbm, down_ref)):
        copy.wait()
    rest = jnp.zeros((PIECE, DENSE_COLS - 3 * SHARE), F32)
    wide = [ref[...].astype(F32) for ref in (gate_ref, up_ref, down_ref)]
    first = jnp.concatenate([w[:, :SHARE] for w in wide] + [rest], axis=1).astype(BF16)
    second = jnp.concatenate([w[:, SHARE:] for w in wide] + [rest], axis=1).astype(BF16)

    @pl.when(low[0] == 0)
    def _():
        own_ref[...] = first
        near_ref[...] = second

    @pl.when(low[0] != 0)
    def _():
        own_ref[...] = second
        near_ref[...] = first


def dense_kernel(core, *refs):
    own_ref, own_grad_ref, near_m, near_o, *pieces = refs[: 4 + PIECES]
    _, out_mine_ref, out_other_ref, weights, rows, grads, sems = refs[4 + PIECES :]
    at = halves(core)
    near = pl.ds(ROWS, ROWS)
    copies = []

    def copy(source, target):
        copies.append(pltpu.make_async_copy(source, target, sems.at[len(copies)]))
        copies[-1].start()

    copy(own_ref, rows.at[pl.ds(0, ROWS), :])
    copy(own_grad_ref, grads.at[pl.ds(0, ROWS), :])
    for h, ref in enumerate((near_m, near_o)):
        copy(ref.at[pl.ds(0, ROWS), :], rows.at[near, pl.ds(at[h], HALF)])
        copy(ref.at[near, :], grads.at[near, pl.ds(at[h], HALF)])
    for n, (piece, line, *_) in enumerate(PLACES):
        start = pl.multiple_of(core[1 + n], PIECE)
        copy(pieces[piece].at[pl.ds(line, PIECE), :], weights.at[pl.ds(start, PIECE), :])
    for one in copies:
        one.wait()
    pre = dot(rows[...], weights[:, : 2 * SHARE])
    gate_pre, up_pre = pre[:, :SHARE], pre[:, SHARE:]
    hidden_grad = dot(grads[...], weights[:, 512:])[:, 2 * SHARE - 512 : 3 * SHARE - 512]
    activated, slope = silu_parts(gate_pre)
    zeros = lambda n: jnp.zeros((2 * ROWS, n), F32)
    hidden = jnp.concatenate([zeros(2 * SHARE - 512), activated * up_pre, zeros(DENSE_COLS - 3 * SHARE)], axis=1)
    hidden = hidden.astype(BF16)
    pre_grad = jnp.concatenate([hidden_grad * up_pre * slope, hidden_grad * activated], axis=1).astype(BF16)
    for h, ref in ((1, out_other_ref), (0, out_mine_ref)):
        part = pl.ds(at[h], HALF)
        forward = dot_last(hidden, weights[part, 512:]).astype(BF16)
        ref[:ROWS, :] = forward[:ROWS]
        ref[2 * ROWS : 3 * ROWS, :] = forward[ROWS:]
        backward = dot_last(pre_grad, weights[part, : 2 * SHARE]).astype(BF16)
        ref[ROWS : 2 * ROWS, :] = backward[:ROWS]
        ref[3 * ROWS :, :] = backward[ROWS:]


def picked_rows(found, packed):
    first, low, high = found
    rest = packed[:, HALF:]
    return dot(first, packed[:, :HALF]) + jnp.concatenate([dot(low, rest), dot(high, rest)], axis=1)


def thirds(column):
    lanes = lax.broadcasted_iota(I32, (ROWS, 128), 1)
    high = column.astype(BF16).astype(F32)
    middle = (column - high).astype(BF16).astype(F32)
    low = column - high - middle
    return jnp.where(lanes == 0, high, jnp.where(lanes == 1, middle, jnp.where(lanes == 2, low, 0.0))).astype(BF16)


def total(columns):
    return jnp.sum(columns.astype(F32), axis=1, keepdims=True)


def combine(core, routes_ref, back_ref, dense_refs, small_hbm, features_hbm, bufs, sems, first):
    dense, small, features = bufs
    rows = pl.ds(first, ROWS)
    mine = pl.ds(halves(core)[0], HALF)
    sources = [dense_refs[0].at[rows, :], dense_refs[1].at[rows, :], dense_refs[2]]
    copies = begin(
        sems,
        *[(source, dense.at[n]) for n, source in enumerate(sources)],
        (small_hbm, small),
        (features_hbm.at[:, mine], features),
    )
    found = place_marks(routes_of(routes_ref))
    one, two = (picked_rows(found[k], back_ref[...]) for k in range(2))
    for copy in copies:
        copy.wait()
    gate = small[:, 1:2]
    part = dense[0].astype(F32) + dense[1].astype(F32) + dense[2].astype(F32)
    return one, two, part + gate * one + (1.0 - gate) * two


def combine_forward_kernel(
    core, routes_ref, back_ref, dense_a, dense_b, dense_c, small_ref, grad_ref, out_ref, dense, small, grad, sems
):
    one, two, part = combine(
        core, routes_ref, back_ref, (dense_a, dense_b, dense_c), small_ref, grad_ref, (dense, small, grad), sems, 0
    )
    out_ref[:, :HALF] = part.astype(BF16)
    out_ref[:, HALF:] = thirds(jnp.sum(grad[...].astype(F32) * (one - two), axis=1, keepdims=True))


def combine_backward_kernel(
    core, routes_ref, back_ref, dense_a, dense_b, dense_c, small_ref, tokens_ref, gain_ref, out_ref,
    dense, small, tokens, sems,
):
    _, _, part = combine(
        core, routes_ref, back_ref, (dense_a, dense_b, dense_c), small_ref, tokens_ref, (dense, small, tokens), sems, ROWS
    )
    out_ref[:, :HALF] = part.astype(BF16)
    weighted = tokens[...].astype(F32) * gain_ref[:, pl.ds(halves(core)[0], HALF)] * part
    out_ref[:, HALF:] = thirds(jnp.sum(weighted, axis=1, keepdims=True))


def add_far_kernel(core, forward_ref, forward_far_ref, back_ref, back_far_ref, tokens_ref, out_ref):
    layer = tokens_ref[:, pl.ds(halves(core)[0], HALF)].astype(F32) + (
        forward_ref[:, :HALF].astype(F32) + forward_far_ref[:, :HALF].astype(F32)
    )
    out_ref[:ROWS, :HALF] = layer.astype(BF16)
    out_ref[ROWS:, :HALF] = (back_ref[:, :HALF].astype(F32) + back_far_ref[:, :HALF].astype(F32)).astype(BF16)
    out_ref[:ROWS, HALF:] = thirds(total(forward_ref[:, HALF:]) + total(forward_far_ref[:, HALF:]))
    out_ref[ROWS:, HALF:] = thirds(total(back_ref[:, HALF:]) + total(back_far_ref[:, HALF:]))


def finish_kernel(
    core, routes_ref, mine_ref, other_ref, small_ref, tokens_ref, grad_ref, gain_ref, router_ref,
    layer_ref, grad_in_ref,
):
    scale, gate, leaning = small_ref[:, 0:1], small_ref[:, 1:2], small_ref[:, 2:3]
    dots, sums = (
        total(mine_ref[rows, HALF:]) + total(other_ref[rows, HALF:]) for rows in (slice(0, ROWS), slice(ROWS, None))
    )
    logit_grad = gate * (1.0 - gate) * dots
    mean = scale * scale * scale * ((sums + logit_grad * leaning) / D)
    marks = marks_of(routes_of(routes_ref))
    difference = (marks[0] - marks[1]).astype(BF16)
    at = halves(core)
    for h, ref in enumerate((mine_ref, other_ref)):
        part = pl.ds(at[h], HALF)
        layer_ref[:, part] = ref[:ROWS, :HALF]
        grown = ref[ROWS:, :HALF].astype(F32) + logit_grad * dot(difference, router_ref[:, part])
        moved = scale * (grown * gain_ref[:, part]) - tokens_ref[:, part].astype(F32) * mean
        grad_in_ref[:, part] = (grad_ref[:, part].astype(F32) + moved).astype(BF16)


def exchange(packed):
    blocks = packed.reshape(EXPERTS, 8, packed.shape[1])
    return lax.all_to_all(blocks, "expert", split_axis=0, concat_axis=0, tiled=True).reshape(packed.shape)


PIECES = 8


PLACES = [
    (n, (2 * k + side) * PIECE, side, 2 * (n % 2) + k, n // 2)
    for n in range(PIECES)
    for k in range(2)
    for side in range(2)
]


def shards(
    tokens, norm_gain, router, expert_gate, expert_up, expert_down,
    dense_gate, dense_up, dense_down_t, routes, grad_out,
):
    index = lax.axis_index("expert")
    core_index = lax.axis_index("tensor") % 2
    x_lo, y, z = index // 16, (index // 4) % 4, index % 4
    core = core_index.astype(I32).reshape(1)
    gain = norm_gain.reshape(1, D)
    w_gate, w_up, w_down = expert_gate[0], expert_up[0], expert_down[0]

    full = lambda array: (array, False)
    raw = lambda array: (array, True)
    hbm = lambda *shape: (shape, BF16, True)
    kept = lambda *shape: (shape, BF16, False)

    routes = routes.T
    router = router.T

    packed, normed, scale, share = call(
        dispatch_kernel,
        [full(routes), full(tokens), full(gain), full(grad_out)],
        [hbm(LINES, 2 * PACKED), hbm(ROWS, D), ((ROWS, 128), F32, True), hbm(2 * ROWS, HALF)],
        core=core,
        takes=7,
    )

    own_weights, near_weights = call(
        split_weights_kernel,
        [raw(dense_gate), raw(dense_up), raw(dense_down_t)],
        [kept(PIECE, DENSE_COLS)] * 2,
        [pltpu.VMEM((PIECE, HID), BF16)] * 3 + [pltpu.SemaphoreType.DMA((3,))],
        core=x_lo.astype(I32).reshape(1),
    )
    pair = jnp.concatenate([own_weights, send(near_weights, SWAP_XLO)], axis=0)
    packed, pair = lax.optimization_barrier((packed, pair))
    (small,) = call(
        gates_kernel,
        [full(routes), full(tokens), full(gain), full(router), full(normed), full(scale)],
        [((ROWS, 128), F32, True)],
        core=core,
        takes=40,
    )
    arrived, near_mine, small, *around = lax.optimization_barrier(
        (exchange(packed), send(share, TO_X), small, *[send(pair, across(n, True)) for n in (1, 2, 3)])
    )
    low, high = jnp.concatenate([pair, around[0]], axis=0), jnp.concatenate(around[1:], axis=0)
    low_after, high_ahead = send(low, across(1, False)), send(high, across(3, False))
    high_after, low_ahead = send(high, across(1, False)), send(low, across(3, False))

    near_other = send(near_mine, SWAP_CORE)

    arrived_other = send(arrived, SWAP_CORE)
    weights = [raw(w_gate), raw(w_up), raw(w_down)]
    buffers = [pltpu.VMEM((D, HID), BF16), pltpu.VMEM((D, HID), BF16), pltpu.VMEM((HID, D), BF16)]
    buffers += [pltpu.VMEM((SLOTS, HID), F32)] * 2 + [pltpu.VMEM((2, SLOTS, HALF), BF16)]
    result_mine, result_other, gate_pre, up_pre = call(
        expert_forward_kernel,
        [full(arrived), full(arrived_other), *weights],
        [hbm(LINES, PACKED), kept(LINES, PACKED)] + [((SLOTS, HID), F32, "copied")] * 2,
        buffers + [pltpu.SemaphoreType.DMA((8,))],
        core,
        takes=14,
        limit=40,
    )
    result_mine, result_other, low_after, high_ahead, high_after, low_ahead, near_other = lax.optimization_barrier(
        (result_mine, result_other, low_after, high_ahead, high_after, low_ahead, near_other)
    )
    low_far, high_far = send(low_after, across(1, False)), send(high_ahead, across(3, False))

    def joined(mine, other):
        return (mine.astype(F32) + send(other, SWAP_CORE).astype(F32)).astype(BF16)

    result = joined(result_mine, result_other)
    back_result = exchange(result)
    grads_mine, grads_other = call(
        expert_backward_kernel,
        [raw(arrived), raw(arrived_other), raw(gate_pre), raw(up_pre), *weights, raw(result)],
        [hbm(LINES, PACKED), kept(LINES, PACKED)],
        buffers + [pltpu.VMEM((2, LINES, PACKED), BF16), pltpu.SemaphoreType.DMA((10,))],
        core,
        takes=14,
        limit=40,
    )

    def start_of(side, first, second):
        dy, dz = jnp.where(core_index == 0, second, first), jnp.where(core_index == 0, first, second)
        return (((x_lo + side) % 2 * 4 + (y - dy) % 4) * 4 + (z - dz) % 4) * PIECE

    table = jnp.array([place[2:] for place in PLACES], I32)
    starts = start_of(table[:, 0], table[:, 1], table[:, 2]).astype(I32)

    pieces = [low, high, low_after, high_after, low_far, high_far, low_ahead, high_ahead]
    dense_mine, dense_other = call(
        dense_kernel,
        [raw(a) for a in (normed, grad_out, near_mine, near_other, *pieces, grads_other)],
        [hbm(4 * ROWS, HALF), kept(4 * ROWS, HALF)],
        [
            pltpu.VMEM((D, DENSE_COLS), BF16),
            pltpu.VMEM((2 * ROWS, D), BF16),
            pltpu.VMEM((2 * ROWS, D), BF16),
            pltpu.SemaphoreType.DMA((6 + len(PLACES),)),
        ],
        jnp.concatenate([core, starts]),
        takes=12,
        limit=28,
    )
    dense_other, back_result = lax.optimization_barrier((dense_other, back_result))
    dense_far = send(dense_other, SWAP_CORE)
    near_sums = [
        (dense_mine[a : a + ROWS].astype(F32) + dense_far[a : a + ROWS].astype(F32)).astype(BF16)
        for a in (2 * ROWS, 3 * ROWS)
    ]
    grads, *near_sums = lax.optimization_barrier((joined(grads_mine, grads_other), *near_sums))
    back_grads = exchange(grads)

    near_far = [send(near_sum, TO_X) for near_sum in near_sums]

    def dense_part(n):
        return [raw(dense_mine), raw(dense_far), raw(near_far[n])]

    row_buffers = [pltpu.VMEM((3, ROWS, HALF), BF16), pltpu.VMEM((ROWS, 128), F32), pltpu.VMEM((ROWS, HALF), BF16)]
    row_buffers += [pltpu.SemaphoreType.DMA((5,))]
    (forward,) = call(
        combine_forward_kernel,
        [full(routes), full(back_result), *dense_part(0), raw(small), raw(grad_out)],
        [kept(ROWS, HALF + 128)],
        row_buffers,
        core=core,
        takes=9,
    )
    forward, near_far[1] = lax.optimization_barrier((forward, near_far[1]))
    forward_far = send(forward, SWAP_XHI)
    forward_far, back_grads = lax.optimization_barrier((forward_far, back_grads))
    (backward,) = call(
        combine_backward_kernel,
        [full(routes), full(back_grads), *dense_part(1), raw(small), raw(tokens), full(gain)],
        [kept(ROWS, HALF + 128)],
        row_buffers,
        core=core,
    )
    backward_far = send(backward, SWAP_XHI)
    (mine,) = call(
        add_far_kernel,
        [full(forward), full(forward_far), full(backward), full(backward_far), full(tokens)],
        [kept(2 * ROWS, HALF + 128)],
        core=core,
    )
    return tuple(
        call(
            finish_kernel,
            [full(routes), full(mine), full(send(mine, SWAP_CORE)), full(small)]
            + [full(tokens), full(grad_out), full(gain), full(router)],
            [kept(ROWS, D)] * 2,
            core=core,
        )
    )


def solution(mesh):
    return jax.shard_map(
        shards,
        mesh=mesh,
        in_specs=(
            P("expert", None),
            P(),
            P(),
            P("expert", None, "tensor"),
            P("expert", None, "tensor"),
            P("expert", "tensor", None),
            P("expert", "tensor"),
            P("expert", "tensor"),
            P("expert", "tensor"),
            P("expert", None),
            P("expert", None),
        ),
        out_specs=(P("expert", None), P("expert", None)),
        check_vma=False,
    )
```

```python
import itertools

import jax
import jax.numpy as jnp
from jax import lax
from jax.experimental import pallas as pl
from jax.experimental.pallas import tpu as pltpu
from jax.sharding import PartitionSpec as P

NORM_EPS = 1e-05
F32, BF16, I32 = jnp.float32, jnp.bfloat16, jnp.int32
EXPERTS = 32
ROWS = 128
D = 3584
HALF = D // 2
QUARTER = D // 4
HID = 640
PACKED = HALF + QUARTER
LINES = EXPERTS * 8
SHARE = HID // 2
DENSE_COLS = 1024
PIECE = 112
DEVICES = ("expert", "tensor")


def permutation(move):
    sizes = (2, 4, 4, 2, 2)

    def flat(place):
        number = 0
        for at, size in zip(place, sizes):
            number = number * size + at % size
        return number

    return [(flat(p), flat(move(*p))) for p in itertools.product(*map(range, sizes))]


def along_x(xl, y, z, xh, core):
    x = (xh * 2 + xl + (1 if xl else -1)) % 4
    return (x % 2, y, z, x // 2, core)


SWAP_CORE = permutation(lambda xl, y, z, xh, c: (xl, y, z, xh, 1 - c))
SWAP_XHI = permutation(lambda xl, y, z, xh, c: (xl, y, z, 1 - xh, c))
SWAP_XLO = permutation(lambda xl, y, z, xh, c: (1 - xl, y, z, xh, c))
TO_X = permutation(along_x)


def send(value, pairs):
    return lax.ppermute(value, DEVICES, pairs)


def across(step, first):
    def move(xl, y, z, xh, c):
        return (xl, y, z + step, xh, c) if (c == 0) == first else (xl, y + step, z, xh, c)

    return permutation(move)


def dot(left, right, dims=((1,), (0,))):
    return lax.dot_general(left, right, (dims, ((), ())), preferred_element_type=F32)


def dot_last(left, right):
    return dot(left, right, ((1,), (1,)))


def silu_parts(pre):
    sigma = 1.0 / (1.0 + jnp.exp(-pre))
    return (pre * sigma, sigma * (1.0 + pre * (1.0 - sigma)))


def call(kernel, ins, outs, scratch=(), core=None, takes=3, limit=16):
    place = lambda raw: pl.BlockSpec(memory_space=pl.ANY if raw else pltpu.VMEM)
    return pl.pallas_call(
        kernel,
        in_specs=[pl.BlockSpec(memory_space=pltpu.SMEM)] + [place(raw) for _, raw in ins],
        out_specs=[place(raw == "copied") for _, _, raw in outs],
        scratch_shapes=list(scratch),
        out_shape=[
            pltpu.HBM(shape, dtype) if raw else jax.ShapeDtypeStruct(shape, dtype) for shape, dtype, raw in outs
        ],
        compiler_params=pltpu.CompilerParams(vmem_limit_bytes=limit * 1024 * 1024),
        cost_estimate=pl.CostEstimate(flops=takes * 1_150_000_000, transcendentals=0, bytes_accessed=takes * 3_000_000),
    )(core, *[pltpu.with_memory_space_constraint(array, pltpu.HBM) if raw else array for array, raw in ins])


def begin(sems, *copies):
    begun = [pltpu.make_async_copy(source, target, sems.at[n]) for n, (source, target) in enumerate(copies)]
    for copy in begun:
        copy.start()
    return begun


def halves(core):
    return [pl.multiple_of(core[0] * HALF, HALF), pl.multiple_of((1 - core[0]) * HALF, HALF)]


def routes_of(ref):
    same = lax.broadcasted_iota(I32, (ROWS, ROWS), 0) == lax.broadcasted_iota(I32, (ROWS, ROWS), 1)
    return dot_last(same.astype(F32).astype(BF16), ref[...].astype(F32).astype(BF16)).astype(I32)


def marks_of(routes):
    lanes = lax.broadcasted_iota(I32, (ROWS, EXPERTS), 1)
    return [(routes[:, k : k + 1] == lanes).astype(F32) for k in range(2)]


def place_marks(routes):
    marks = marks_of(routes)
    earlier = (
        lax.broadcasted_iota(I32, (ROWS, ROWS), 1) < lax.broadcasted_iota(I32, (ROWS, ROWS), 0)
    ).astype(BF16)
    before = dot(earlier, (marks[0] + marks[1]).astype(BF16))
    lines = lax.broadcasted_iota(I32, (ROWS, LINES), 1)
    found = []
    for k in range(2):
        slot = jnp.sum(before * marks[k], axis=1, keepdims=True).astype(I32)
        line = routes[:, k : k + 1] * 8 + slot
        first = (slot < 8) & (lines == line)
        low = (slot >= 8) & (lines == line - 8)
        high = (slot >= 8) & (lines == line - 4)
        found.append([m.astype(F32).astype(BF16) for m in (first, low, high)])
    return found


def pack_by_marks(found, rows, out_ref, at):
    first, low, high = (found[0][i] + found[1][i] for i in range(3))
    down = ((0,), (0,))
    rest = dot(low, rows[:, :QUARTER], down) + dot(high, rows[:, QUARTER:], down)
    out_ref[:, at : at + HALF] = dot(first, rows, down).astype(BF16)
    out_ref[:, at + HALF : at + PACKED] = rest.astype(BF16)


def dispatch_kernel(
    core, routes_ref, tokens_ref, gain_ref, grad_ref, out_ref, normed_ref, scale_ref, share_ref,
):
    routes = routes_of(routes_ref)
    wide = tokens_ref[...].astype(F32)
    scale = lax.rsqrt(jnp.sum(wide * wide, axis=1, keepdims=True) / D + NORM_EPS)
    normed = (wide * scale * gain_ref[...]).astype(BF16)
    normed_ref[...] = normed
    mine = pl.ds(halves(core)[0], HALF)
    part, grad_part = normed_ref[:, mine], grad_ref[:, mine]
    found = place_marks(routes)
    pack_by_marks(found, part, out_ref, 0)
    pack_by_marks(found, grad_part, out_ref, PACKED)
    share_ref[:ROWS, :] = part
    share_ref[ROWS:, :] = grad_part
    scale_ref[...] = jnp.broadcast_to(scale, (ROWS, 128))


def gates_kernel(core, routes_ref, tokens_ref, gain_ref, router_ref, normed_ref, scale_ref, small_ref):
    wide, normed, scale = tokens_ref[...].astype(F32), normed_ref[...], scale_ref[:, 0:1]
    logits = dot_last(normed, router_ref[...])
    marks = marks_of(routes_of(routes_ref))
    picked = [jnp.sum(m * logits, axis=1, keepdims=True) for m in marks]
    gate = 1.0 / (1.0 + jnp.exp(picked[1] - picked[0]))
    difference = dot((marks[0] - marks[1]).astype(BF16), router_ref[...])
    leaning = jnp.sum(wide * gain_ref[...] * difference, axis=1, keepdims=True)
    lanes = lax.broadcasted_iota(I32, (ROWS, 128), 1)
    small_ref[...] = jnp.where(lanes == 0, scale, jnp.where(lanes == 1, gate, leaning))


def spread_marks():
    q = lax.broadcasted_iota(I32, (ROWS, LINES), 0)
    r = lax.broadcasted_iota(I32, (ROWS, LINES), 1)
    qt = lax.broadcasted_iota(I32, (LINES, ROWS), 1)
    rt = lax.broadcasted_iota(I32, (LINES, ROWS), 0)
    ones = lambda m: m.astype(F32).astype(BF16)
    base, base_t = 2 * q - (q & 3), 2 * qt - (qt & 3)
    return (ones(r == base), ones(r == base + 4)), (ones(rt == base_t), ones(rt == base_t + 4))


def unpack(packed, rows_ref):
    (low, high), _ = spread_marks()
    rows_ref[:LINES, :] = packed[:, :HALF]
    rows_ref[LINES:, :QUARTER] = dot(low, packed[:, HALF:]).astype(BF16)
    rows_ref[LINES:, QUARTER:] = dot(high, packed[:, HALF:]).astype(BF16)


def pack(rows, out_ref):
    _, (low, high) = spread_marks()
    out_ref[:, :HALF] = rows[:LINES].astype(BF16)
    rest = rows[LINES:].astype(BF16)
    out_ref[:, HALF:] = (dot(low, rest[:, :QUARTER]) + dot(high, rest[:, QUARTER:])).astype(BF16)


SLOTS = EXPERTS * 12


def expert_forward_kernel(
    core, mine_ref, other_ref, gate_hbm, up_hbm, down_hbm,
    out_mine_ref, out_other_ref, gate_pre_hbm, up_pre_hbm,
    gate_ref, up_ref, down_ref, gate_pre_ref, up_pre_ref, rows, sems,
):
    at = halves(core)
    parts = [pl.ds(at[h], HALF) for h in range(2)]
    gate = begin(sems.at[pl.ds(0, 2)], *[(gate_hbm.at[p, :], gate_ref.at[p, :]) for p in parts])
    for h, ref in enumerate((mine_ref, other_ref)):
        unpack(ref[:, :PACKED], rows.at[h])
    up = begin(sems.at[pl.ds(2, 2)], *[(up_hbm.at[p, :], up_ref.at[p, :]) for p in parts])
    gate[0].wait()
    product = dot(rows[0], gate_ref[parts[0], :])
    gate[1].wait()
    gate_pre_ref[...] = product + dot(rows[1], gate_ref[parts[1], :])
    down = begin(sems.at[pl.ds(4, 2)], *[(down_hbm.at[:, p], down_ref.at[:, p]) for p in reversed(parts)])
    up[0].wait()
    product = dot(rows[0], up_ref[parts[0], :])
    up[1].wait()
    up_pre_ref[...] = product + dot(rows[1], up_ref[parts[1], :])
    written = begin(sems.at[pl.ds(6, 2)], (gate_pre_ref, gate_pre_hbm), (up_pre_ref, up_pre_hbm))
    activated, _ = silu_parts(gate_pre_ref[...])
    hidden = (activated * up_pre_ref[...]).astype(BF16)
    for n, (h, ref) in enumerate(((1, out_other_ref), (0, out_mine_ref))):
        down[n].wait()
        pack(dot(hidden, down_ref[:, parts[h]]), ref)
    for copy in written:
        copy.wait()


def expert_backward_kernel(
    core, mine_hbm, other_hbm, gate_pre_hbm, up_pre_hbm, gate_hbm, up_hbm, down_hbm, after_ref,
    out_mine_ref, out_other_ref,
    gate_ref, up_ref, down_ref, gate_pre_ref, up_pre_ref, rows, arrived, sems,
):
    del after_ref
    at = halves(core)
    parts = [pl.ds(at[h], HALF) for h in range(2)]
    last = pl.ds(PACKED, PACKED)
    incoming = begin(
        sems.at[pl.ds(0, 4)],
        *[
            copy
            for h, ref in enumerate((mine_hbm, other_hbm))
            for copy in ((ref.at[:, last], arrived.at[h]), (down_hbm.at[:, parts[h]], down_ref.at[:, parts[h]]))
        ],
    )
    hidden_grad = 0.0
    for h in range(2):
        incoming[2 * h].wait()
        unpack(arrived[h], rows.at[h])
        incoming[2 * h + 1].wait()
        if h == 0:
            pre = begin(sems.at[pl.ds(4, 2)], (gate_pre_hbm, gate_pre_ref), (up_pre_hbm, up_pre_ref))
            weights = begin(
                sems.at[pl.ds(6, 4)],
                *[
                    copy
                    for p in reversed(parts)
                    for copy in ((gate_hbm.at[p, :], gate_ref.at[p, :]), (up_hbm.at[p, :], up_ref.at[p, :]))
                ],
            )
        hidden_grad = hidden_grad + dot_last(rows[h], down_ref[:, parts[h]])
    for copy in pre:
        copy.wait()
    activated, slope = silu_parts(gate_pre_ref[...])
    gate_grad = (hidden_grad * up_pre_ref[...] * slope).astype(BF16)
    up_grad = (hidden_grad * activated).astype(BF16)
    for n, (h, ref) in enumerate(((1, out_other_ref), (0, out_mine_ref))):
        weights[2 * n].wait()
        product = dot_last(gate_grad, gate_ref[parts[h], :])
        weights[2 * n + 1].wait()
        pack(product + dot_last(up_grad, up_ref[parts[h], :]), ref)


def split_weights_kernel(low, gate_hbm, up_hbm, down_hbm, own_ref, near_ref, gate_ref, up_ref, down_ref, sems):
    for copy in begin(sems, (gate_hbm, gate_ref), (up_hbm, up_ref), (down_hbm, down_ref)):
        copy.wait()
    rest = jnp.zeros((PIECE, DENSE_COLS - 3 * SHARE), F32)
    wide = [ref[...].astype(F32) for ref in (gate_ref, up_ref, down_ref)]
    first = jnp.concatenate([w[:, :SHARE] for w in wide] + [rest], axis=1).astype(BF16)
    second = jnp.concatenate([w[:, SHARE:] for w in wide] + [rest], axis=1).astype(BF16)

    @pl.when(low[0] == 0)
    def _():
        own_ref[...] = first
        near_ref[...] = second

    @pl.when(low[0] != 0)
    def _():
        own_ref[...] = second
        near_ref[...] = first


def dense_kernel(core, *refs):
    own_ref, own_grad_ref, near_m, near_o, *pieces = refs[: 4 + PIECES]
    _, out_mine_ref, out_other_ref, weights, rows, grads, sems = refs[4 + PIECES :]
    at = halves(core)
    near = pl.ds(ROWS, ROWS)
    copies = []

    def copy(source, target):
        copies.append(pltpu.make_async_copy(source, target, sems.at[len(copies)]))
        copies[-1].start()

    copy(own_ref, rows.at[pl.ds(0, ROWS), :])
    copy(own_grad_ref, grads.at[pl.ds(0, ROWS), :])
    for h, ref in enumerate((near_m, near_o)):
        copy(ref.at[pl.ds(0, ROWS), :], rows.at[near, pl.ds(at[h], HALF)])
        copy(ref.at[near, :], grads.at[near, pl.ds(at[h], HALF)])
    for n, (piece, line, *_) in enumerate(PLACES):
        start = pl.multiple_of(core[1 + n], PIECE)
        copy(pieces[piece].at[pl.ds(line, PIECE), :], weights.at[pl.ds(start, PIECE), :])
    for one in copies:
        one.wait()
    pre = dot(rows[...], weights[:, : 2 * SHARE])
    gate_pre, up_pre = pre[:, :SHARE], pre[:, SHARE:]
    hidden_grad = dot(grads[...], weights[:, 512:])[:, 2 * SHARE - 512 : 3 * SHARE - 512]
    activated, slope = silu_parts(gate_pre)
    zeros = lambda n: jnp.zeros((2 * ROWS, n), F32)
    hidden = jnp.concatenate([zeros(2 * SHARE - 512), activated * up_pre, zeros(DENSE_COLS - 3 * SHARE)], axis=1)
    hidden = hidden.astype(BF16)
    pre_grad = jnp.concatenate([hidden_grad * up_pre * slope, hidden_grad * activated], axis=1).astype(BF16)
    for h, ref in ((1, out_other_ref), (0, out_mine_ref)):
        part = pl.ds(at[h], HALF)
        forward = dot_last(hidden, weights[part, 512:]).astype(BF16)
        ref[:ROWS, :] = forward[:ROWS]
        ref[2 * ROWS : 3 * ROWS, :] = forward[ROWS:]
        backward = dot_last(pre_grad, weights[part, : 2 * SHARE]).astype(BF16)
        ref[ROWS : 2 * ROWS, :] = backward[:ROWS]
        ref[3 * ROWS :, :] = backward[ROWS:]


def picked_rows(found, packed):
    first, low, high = found
    rest = packed[:, HALF:]
    return dot(first, packed[:, :HALF]) + jnp.concatenate([dot(low, rest), dot(high, rest)], axis=1)


def thirds(column):
    lanes = lax.broadcasted_iota(I32, (ROWS, 128), 1)
    high = column.astype(BF16).astype(F32)
    middle = (column - high).astype(BF16).astype(F32)
    low = column - high - middle
    return jnp.where(lanes == 0, high, jnp.where(lanes == 1, middle, jnp.where(lanes == 2, low, 0.0))).astype(BF16)


def total(columns):
    return jnp.sum(columns.astype(F32), axis=1, keepdims=True)


def combine(core, routes_ref, back_ref, dense_refs, small_hbm, features_hbm, bufs, sems, first):
    dense, small, features = bufs
    rows = pl.ds(first, ROWS)
    mine = pl.ds(halves(core)[0], HALF)
    sources = [dense_refs[0].at[rows, :], dense_refs[1].at[rows, :], dense_refs[2]]
    copies = begin(
        sems,
        *[(source, dense.at[n]) for n, source in enumerate(sources)],
        (small_hbm, small),
        (features_hbm.at[:, mine], features),
    )
    found = place_marks(routes_of(routes_ref))
    one, two = (picked_rows(found[k], back_ref[...]) for k in range(2))
    for copy in copies:
        copy.wait()
    gate = small[:, 1:2]
    part = dense[0].astype(F32) + dense[1].astype(F32) + dense[2].astype(F32)
    return one, two, part + gate * one + (1.0 - gate) * two


def combine_forward_kernel(
    core, routes_ref, back_ref, dense_a, dense_b, dense_c, small_ref, grad_ref, out_ref, dense, small, grad, sems
):
    one, two, part = combine(
        core, routes_ref, back_ref, (dense_a, dense_b, dense_c), small_ref, grad_ref, (dense, small, grad), sems, 0
    )
    out_ref[:, :HALF] = part.astype(BF16)
    out_ref[:, HALF:] = thirds(jnp.sum(grad[...].astype(F32) * (one - two), axis=1, keepdims=True))


def combine_backward_kernel(
    core, routes_ref, back_ref, dense_a, dense_b, dense_c, small_ref, tokens_ref, gain_ref, out_ref,
    dense, small, tokens, sems,
):
    _, _, part = combine(
        core, routes_ref, back_ref, (dense_a, dense_b, dense_c), small_ref, tokens_ref, (dense, small, tokens), sems, ROWS
    )
    out_ref[:, :HALF] = part.astype(BF16)
    weighted = tokens[...].astype(F32) * gain_ref[:, pl.ds(halves(core)[0], HALF)] * part
    out_ref[:, HALF:] = thirds(jnp.sum(weighted, axis=1, keepdims=True))


def add_far_kernel(core, forward_ref, forward_far_ref, back_ref, back_far_ref, tokens_ref, out_ref):
    layer = tokens_ref[:, pl.ds(halves(core)[0], HALF)].astype(F32) + (
        forward_ref[:, :HALF].astype(F32) + forward_far_ref[:, :HALF].astype(F32)
    )
    out_ref[:ROWS, :HALF] = layer.astype(BF16)
    out_ref[ROWS:, :HALF] = (back_ref[:, :HALF].astype(F32) + back_far_ref[:, :HALF].astype(F32)).astype(BF16)
    out_ref[:ROWS, HALF:] = thirds(total(forward_ref[:, HALF:]) + total(forward_far_ref[:, HALF:]))
    out_ref[ROWS:, HALF:] = thirds(total(back_ref[:, HALF:]) + total(back_far_ref[:, HALF:]))


def finish_kernel(
    core, routes_ref, mine_ref, other_ref, small_ref, tokens_ref, grad_ref, gain_ref, router_ref,
    layer_ref, grad_in_ref,
):
    scale, gate, leaning = small_ref[:, 0:1], small_ref[:, 1:2], small_ref[:, 2:3]
    dots, sums = (
        total(mine_ref[rows, HALF:]) + total(other_ref[rows, HALF:]) for rows in (slice(0, ROWS), slice(ROWS, None))
    )
    logit_grad = gate * (1.0 - gate) * dots
    mean = scale * scale * scale * ((sums + logit_grad * leaning) / D)
    marks = marks_of(routes_of(routes_ref))
    difference = (marks[0] - marks[1]).astype(BF16)
    at = halves(core)
    for h, ref in enumerate((mine_ref, other_ref)):
        part = pl.ds(at[h], HALF)
        layer_ref[:, part] = ref[:ROWS, :HALF]
        grown = ref[ROWS:, :HALF].astype(F32) + logit_grad * dot(difference, router_ref[:, part])
        moved = scale * (grown * gain_ref[:, part]) - tokens_ref[:, part].astype(F32) * mean
        grad_in_ref[:, part] = (grad_ref[:, part].astype(F32) + moved).astype(BF16)


def exchange(packed):
    blocks = packed.reshape(EXPERTS, 8, packed.shape[1])
    return lax.all_to_all(blocks, "expert", split_axis=0, concat_axis=0, tiled=True).reshape(packed.shape)


PIECES = 8


PLACES = [
    (n, (2 * k + side) * PIECE, side, 2 * (n % 2) + k, n // 2)
    for n in range(PIECES)
    for k in range(2)
    for side in range(2)
]


def shards(
    tokens, norm_gain, router, expert_gate, expert_up, expert_down,
    dense_gate, dense_up, dense_down_t, routes, grad_out,
):
    index = lax.axis_index("expert")
    core_index = lax.axis_index("tensor") % 2
    x_lo, y, z = index // 16, (index // 4) % 4, index % 4
    core = core_index.astype(I32).reshape(1)
    gain = norm_gain.reshape(1, D)
    w_gate, w_up, w_down = expert_gate[0], expert_up[0], expert_down[0]

    full = lambda array: (array, False)
    raw = lambda array: (array, True)
    hbm = lambda *shape: (shape, BF16, True)
    kept = lambda *shape: (shape, BF16, False)

    routes = routes.T
    router = router.T

    packed, normed, scale, share = call(
        dispatch_kernel,
        [full(routes), full(tokens), full(gain), full(grad_out)],
        [hbm(LINES, 2 * PACKED), hbm(ROWS, D), ((ROWS, 128), F32, True), hbm(2 * ROWS, HALF)],
        core=core,
        takes=7,
    )

    own_weights, near_weights = call(
        split_weights_kernel,
        [raw(dense_gate), raw(dense_up), raw(dense_down_t)],
        [kept(PIECE, DENSE_COLS)] * 2,
        [pltpu.VMEM((PIECE, HID), BF16)] * 3 + [pltpu.SemaphoreType.DMA((3,))],
        core=x_lo.astype(I32).reshape(1),
    )
    pair = jnp.concatenate([own_weights, send(near_weights, SWAP_XLO)], axis=0)
    packed, pair = lax.optimization_barrier((packed, pair))
    (small,) = call(
        gates_kernel,
        [full(routes), full(tokens), full(gain), full(router), full(normed), full(scale)],
        [((ROWS, 128), F32, True)],
        core=core,
        takes=40,
    )
    arrived, near_mine, small, *around = lax.optimization_barrier(
        (exchange(packed), send(share, TO_X), small, *[send(pair, across(n, True)) for n in (1, 2, 3)])
    )
    low, high = jnp.concatenate([pair, around[0]], axis=0), jnp.concatenate(around[1:], axis=0)
    low_after, high_ahead = send(low, across(1, False)), send(high, across(3, False))
    high_after, low_ahead = send(high, across(1, False)), send(low, across(3, False))

    near_other = send(near_mine, SWAP_CORE)

    arrived_other = send(arrived, SWAP_CORE)
    weights = [raw(w_gate), raw(w_up), raw(w_down)]
    buffers = [pltpu.VMEM((D, HID), BF16), pltpu.VMEM((D, HID), BF16), pltpu.VMEM((HID, D), BF16)]
    buffers += [pltpu.VMEM((SLOTS, HID), F32)] * 2 + [pltpu.VMEM((2, SLOTS, HALF), BF16)]
    result_mine, result_other, gate_pre, up_pre = call(
        expert_forward_kernel,
        [full(arrived), full(arrived_other), *weights],
        [hbm(LINES, PACKED), kept(LINES, PACKED)] + [((SLOTS, HID), F32, "copied")] * 2,
        buffers + [pltpu.SemaphoreType.DMA((8,))],
        core,
        takes=14,
        limit=40,
    )
    result_mine, result_other, low_after, high_ahead, high_after, low_ahead, near_other = lax.optimization_barrier(
        (result_mine, result_other, low_after, high_ahead, high_after, low_ahead, near_other)
    )
    low_far, high_far = send(low_after, across(1, False)), send(high_ahead, across(3, False))

    def joined(mine, other):
        return (mine.astype(F32) + send(other, SWAP_CORE).astype(F32)).astype(BF16)

    result = joined(result_mine, result_other)
    back_result = exchange(result)
    grads_mine, grads_other = call(
        expert_backward_kernel,
        [raw(arrived), raw(arrived_other), raw(gate_pre), raw(up_pre), *weights, raw(result)],
        [hbm(LINES, PACKED), kept(LINES, PACKED)],
        buffers + [pltpu.VMEM((2, LINES, PACKED), BF16), pltpu.SemaphoreType.DMA((10,))],
        core,
        takes=14,
        limit=40,
    )

    def start_of(side, first, second):
        dy, dz = jnp.where(core_index == 0, second, first), jnp.where(core_index == 0, first, second)
        return (((x_lo + side) % 2 * 4 + (y - dy) % 4) * 4 + (z - dz) % 4) * PIECE

    table = jnp.array([place[2:] for place in PLACES], I32)
    starts = start_of(table[:, 0], table[:, 1], table[:, 2]).astype(I32)

    pieces = [low, high, low_after, high_after, low_far, high_far, low_ahead, high_ahead]
    dense_mine, dense_other = call(
        dense_kernel,
        [raw(a) for a in (normed, grad_out, near_mine, near_other, *pieces, grads_other)],
        [hbm(4 * ROWS, HALF), kept(4 * ROWS, HALF)],
        [
            pltpu.VMEM((D, DENSE_COLS), BF16),
            pltpu.VMEM((2 * ROWS, D), BF16),
            pltpu.VMEM((2 * ROWS, D), BF16),
            pltpu.SemaphoreType.DMA((6 + len(PLACES),)),
        ],
        jnp.concatenate([core, starts]),
        takes=12,
        limit=28,
    )
    dense_other, back_result = lax.optimization_barrier((dense_other, back_result))
    dense_far = send(dense_other, SWAP_CORE)
    near_sums = [
        (dense_mine[a : a + ROWS].astype(F32) + dense_far[a : a + ROWS].astype(F32)).astype(BF16)
        for a in (2 * ROWS, 3 * ROWS)
    ]
    grads, *near_sums = lax.optimization_barrier((joined(grads_mine, grads_other), *near_sums))
    back_grads = exchange(grads)

    near_far = [send(near_sum, TO_X) for near_sum in near_sums]

    def dense_part(n):
        return [raw(dense_mine), raw(dense_far), raw(near_far[n])]

    row_buffers = [pltpu.VMEM((3, ROWS, HALF), BF16), pltpu.VMEM((ROWS, 128), F32), pltpu.VMEM((ROWS, HALF), BF16)]
    row_buffers += [pltpu.SemaphoreType.DMA((5,))]
    (forward,) = call(
        combine_forward_kernel,
        [full(routes), full(back_result), *dense_part(0), raw(small), raw(grad_out)],
        [kept(ROWS, HALF + 128)],
        row_buffers,
        core=core,
        takes=9,
    )
    forward, near_far[1] = lax.optimization_barrier((forward, near_far[1]))
    forward_far = send(forward, SWAP_XHI)
    forward, back_grads = lax.optimization_barrier((forward, back_grads))
    (backward,) = call(
        combine_backward_kernel,
        [full(routes), full(back_grads), *dense_part(1), raw(small), raw(tokens), full(gain)],
        [kept(ROWS, HALF + 128)],
        row_buffers,
        core=core,
        takes=1,
    )
    backward, forward_far = lax.optimization_barrier((backward, forward_far))
    backward_far = send(backward, SWAP_XHI)
    (mine,) = call(
        add_far_kernel,
        [full(forward), full(forward_far), full(backward), full(backward_far), full(tokens)],
        [kept(2 * ROWS, HALF + 128)],
        core=core,
    )
    return tuple(
        call(
            finish_kernel,
            [full(routes), full(mine), full(send(mine, SWAP_CORE)), full(small)]
            + [full(tokens), full(grad_out), full(gain), full(router)],
            [kept(ROWS, D)] * 2,
            core=core,
        )
    )


def solution(mesh):
    return jax.shard_map(
        shards,
        mesh=mesh,
        in_specs=(
            P("expert", None),
            P(),
            P(),
            P("expert", None, "tensor"),
            P("expert", None, "tensor"),
            P("expert", "tensor", None),
            P("expert", "tensor"),
            P("expert", "tensor"),
            P("expert", "tensor"),
            P("expert", None),
            P("expert", None),
        ),
        out_specs=(P("expert", None), P("expert", None)),
        check_vma=False,
    )
```

```python
import itertools

import jax
import jax.numpy as jnp
from jax import lax
from jax.experimental import pallas as pl
from jax.experimental.pallas import tpu as pltpu
from jax.sharding import PartitionSpec as P

NORM_EPS = 1e-05
F32, BF16, I32 = jnp.float32, jnp.bfloat16, jnp.int32
EXPERTS = 32
ROWS = 128
D = 3584
HALF = D // 2
QUARTER = D // 4
HID = 640
PACKED = HALF + QUARTER
LINES = EXPERTS * 8
SHARE = HID // 2
DENSE_COLS = 1024
PIECE = 112
DEVICES = ("expert", "tensor")


def permutation(move):
    sizes = (2, 4, 4, 2, 2)

    def flat(place):
        number = 0
        for at, size in zip(place, sizes):
            number = number * size + at % size
        return number

    return [(flat(p), flat(move(*p))) for p in itertools.product(*map(range, sizes))]


def along_x(xl, y, z, xh, core):
    x = (xh * 2 + xl + (1 if xl else -1)) % 4
    return (x % 2, y, z, x // 2, core)


SWAP_CORE = permutation(lambda xl, y, z, xh, c: (xl, y, z, xh, 1 - c))
SWAP_XHI = permutation(lambda xl, y, z, xh, c: (xl, y, z, 1 - xh, c))
SWAP_XLO = permutation(lambda xl, y, z, xh, c: (1 - xl, y, z, xh, c))
TO_X = permutation(along_x)


def send(value, pairs):
    return lax.ppermute(value, DEVICES, pairs)


def across(step, first):
    def move(xl, y, z, xh, c):
        return (xl, y, z + step, xh, c) if (c == 0) == first else (xl, y + step, z, xh, c)

    return permutation(move)


def dot(left, right, dims=((1,), (0,))):
    return lax.dot_general(left, right, (dims, ((), ())), preferred_element_type=F32)


def dot_last(left, right):
    return dot(left, right, ((1,), (1,)))


def silu_parts(pre):
    sigma = 1.0 / (1.0 + jnp.exp(-pre))
    return (pre * sigma, sigma * (1.0 + pre * (1.0 - sigma)))


def call(kernel, ins, outs, scratch=(), core=None, takes=3, limit=16):
    place = lambda raw: pl.BlockSpec(memory_space=pl.ANY if raw else pltpu.VMEM)
    return pl.pallas_call(
        kernel,
        in_specs=[pl.BlockSpec(memory_space=pltpu.SMEM)] + [place(raw) for _, raw in ins],
        out_specs=[place(raw == "copied") for _, _, raw in outs],
        scratch_shapes=list(scratch),
        out_shape=[
            pltpu.HBM(shape, dtype) if raw else jax.ShapeDtypeStruct(shape, dtype) for shape, dtype, raw in outs
        ],
        compiler_params=pltpu.CompilerParams(vmem_limit_bytes=limit * 1024 * 1024),
        cost_estimate=pl.CostEstimate(flops=takes * 1_150_000_000, transcendentals=0, bytes_accessed=takes * 3_000_000),
    )(core, *[pltpu.with_memory_space_constraint(array, pltpu.HBM) if raw else array for array, raw in ins])


def begin(sems, *copies):
    begun = [pltpu.make_async_copy(source, target, sems.at[n]) for n, (source, target) in enumerate(copies)]
    for copy in begun:
        copy.start()
    return begun


def halves(core):
    return [pl.multiple_of(core[0] * HALF, HALF), pl.multiple_of((1 - core[0]) * HALF, HALF)]


def routes_of(ref):
    same = lax.broadcasted_iota(I32, (ROWS, ROWS), 0) == lax.broadcasted_iota(I32, (ROWS, ROWS), 1)
    return dot_last(same.astype(F32).astype(BF16), ref[...].astype(F32).astype(BF16)).astype(I32)


def marks_of(routes):
    lanes = lax.broadcasted_iota(I32, (ROWS, EXPERTS), 1)
    return [(routes[:, k : k + 1] == lanes).astype(F32) for k in range(2)]


def place_marks(routes):
    marks = marks_of(routes)
    earlier = (
        lax.broadcasted_iota(I32, (ROWS, ROWS), 1) < lax.broadcasted_iota(I32, (ROWS, ROWS), 0)
    ).astype(BF16)
    before = dot(earlier, (marks[0] + marks[1]).astype(BF16))
    lines = lax.broadcasted_iota(I32, (ROWS, LINES), 1)
    found = []
    for k in range(2):
        slot = jnp.sum(before * marks[k], axis=1, keepdims=True).astype(I32)
        line = routes[:, k : k + 1] * 8 + slot
        first = (slot < 8) & (lines == line)
        low = (slot >= 8) & (lines == line - 8)
        high = (slot >= 8) & (lines == line - 4)
        found.append([m.astype(F32).astype(BF16) for m in (first, low, high)])
    return found


def pack_by_marks(found, rows, out_ref, at):
    first, low, high = (found[0][i] + found[1][i] for i in range(3))
    down = ((0,), (0,))
    rest = dot(low, rows[:, :QUARTER], down) + dot(high, rows[:, QUARTER:], down)
    out_ref[:, at : at + HALF] = dot(first, rows, down).astype(BF16)
    out_ref[:, at + HALF : at + PACKED] = rest.astype(BF16)


def dispatch_kernel(
    core, routes_ref, tokens_ref, gain_ref, grad_ref, out_ref, normed_ref, scale_ref, share_ref,
):
    routes = routes_of(routes_ref)
    wide = tokens_ref[...].astype(F32)
    scale = lax.rsqrt(jnp.sum(wide * wide, axis=1, keepdims=True) / D + NORM_EPS)
    normed = (wide * scale * gain_ref[...]).astype(BF16)
    normed_ref[...] = normed
    mine = pl.ds(halves(core)[0], HALF)
    part, grad_part = normed_ref[:, mine], grad_ref[:, mine]
    found = place_marks(routes)
    pack_by_marks(found, part, out_ref, 0)
    pack_by_marks(found, grad_part, out_ref, PACKED)
    share_ref[:ROWS, :] = part
    share_ref[ROWS:, :] = grad_part
    scale_ref[...] = jnp.broadcast_to(scale, (ROWS, 128))


def gates_kernel(core, routes_ref, tokens_ref, gain_ref, router_ref, normed_ref, scale_ref, small_ref):
    wide, normed, scale = tokens_ref[...].astype(F32), normed_ref[...], scale_ref[:, 0:1]
    logits = dot_last(normed, router_ref[...])
    marks = marks_of(routes_of(routes_ref))
    picked = [jnp.sum(m * logits, axis=1, keepdims=True) for m in marks]
    gate = 1.0 / (1.0 + jnp.exp(picked[1] - picked[0]))
    difference = dot((marks[0] - marks[1]).astype(BF16), router_ref[...])
    leaning = jnp.sum(wide * gain_ref[...] * difference, axis=1, keepdims=True)
    lanes = lax.broadcasted_iota(I32, (ROWS, 128), 1)
    small_ref[...] = jnp.where(lanes == 0, scale, jnp.where(lanes == 1, gate, leaning))


def spread_marks():
    q = lax.broadcasted_iota(I32, (ROWS, LINES), 0)
    r = lax.broadcasted_iota(I32, (ROWS, LINES), 1)
    qt = lax.broadcasted_iota(I32, (LINES, ROWS), 1)
    rt = lax.broadcasted_iota(I32, (LINES, ROWS), 0)
    ones = lambda m: m.astype(F32).astype(BF16)
    base, base_t = 2 * q - (q & 3), 2 * qt - (qt & 3)
    return (ones(r == base), ones(r == base + 4)), (ones(rt == base_t), ones(rt == base_t + 4))


def unpack(packed, rows_ref):
    (low, high), _ = spread_marks()
    rows_ref[:LINES, :] = packed[:, :HALF]
    rows_ref[LINES:, :QUARTER] = dot(low, packed[:, HALF:]).astype(BF16)
    rows_ref[LINES:, QUARTER:] = dot(high, packed[:, HALF:]).astype(BF16)


def pack(rows, out_ref):
    _, (low, high) = spread_marks()
    out_ref[:, :HALF] = rows[:LINES].astype(BF16)
    rest = rows[LINES:].astype(BF16)
    out_ref[:, HALF:] = (dot(low, rest[:, :QUARTER]) + dot(high, rest[:, QUARTER:])).astype(BF16)


SLOTS = EXPERTS * 12


def expert_forward_kernel(
    core, mine_ref, other_ref, gate_hbm, up_hbm, down_hbm,
    out_mine_ref, out_other_ref, gate_pre_hbm, up_pre_hbm,
    gate_ref, up_ref, down_ref, gate_pre_ref, up_pre_ref, rows, sems,
):
    at = halves(core)
    parts = [pl.ds(at[h], HALF) for h in range(2)]
    gate = begin(sems.at[pl.ds(0, 2)], *[(gate_hbm.at[p, :], gate_ref.at[p, :]) for p in parts])
    for h, ref in enumerate((mine_ref, other_ref)):
        unpack(ref[:, :PACKED], rows.at[h])
    up = begin(sems.at[pl.ds(2, 2)], *[(up_hbm.at[p, :], up_ref.at[p, :]) for p in parts])
    gate[0].wait()
    product = dot(rows[0], gate_ref[parts[0], :])
    gate[1].wait()
    gate_pre_ref[...] = product + dot(rows[1], gate_ref[parts[1], :])
    down = begin(sems.at[pl.ds(4, 2)], *[(down_hbm.at[:, p], down_ref.at[:, p]) for p in reversed(parts)])
    up[0].wait()
    product = dot(rows[0], up_ref[parts[0], :])
    up[1].wait()
    up_pre_ref[...] = product + dot(rows[1], up_ref[parts[1], :])
    written = begin(sems.at[pl.ds(6, 2)], (gate_pre_ref, gate_pre_hbm), (up_pre_ref, up_pre_hbm))
    activated, _ = silu_parts(gate_pre_ref[...])
    hidden = (activated * up_pre_ref[...]).astype(BF16)
    for n, (h, ref) in enumerate(((1, out_other_ref), (0, out_mine_ref))):
        down[n].wait()
        pack(dot(hidden, down_ref[:, parts[h]]), ref)
    for copy in written:
        copy.wait()


def stream(copies, sems, ahead=3):
    started = [pltpu.make_async_copy(source, target, sems.at[n]) for n, (source, target) in enumerate(copies)]
    for copy in started[:ahead]:
        copy.start()
    for n, copy in enumerate(started):
        copy.wait()
        if n + ahead < len(started):
            started[n + ahead].start()
        yield


def quarters(core):
    at = halves(core)
    return [
        (h, pl.ds(q * QUARTER, QUARTER), pl.ds(pl.multiple_of(at[h] + q * QUARTER, QUARTER), QUARTER))
        for h in range(2)
        for q in range(2)
    ]


def pack_quarter(rows, part, out_ref, first):
    _, maps = spread_marks()
    out_ref[:, part] = rows[:LINES].astype(BF16)
    rest = dot(maps[0 if first else 1], rows[LINES:].astype(BF16)).astype(BF16)
    out_ref[:, HALF:] = rest if first else out_ref[:, HALF:] + rest


def expert_backward_kernel(
    core, mine_hbm, other_hbm, gate_pre_hbm, up_pre_hbm, gate_hbm, up_hbm, down_hbm, after_ref,
    out_mine_ref, out_other_ref,
    gate_ref, up_ref, down_ref, gate_pre_ref, up_pre_ref, rows, arrived, sems,
):
    del after_ref
    cut = quarters(core)
    last = pl.ds(PACKED, PACKED)
    copies = []
    for h, ref in enumerate((mine_hbm, other_hbm)):
        copies += [(ref.at[:, last], arrived.at[h])]
        copies += [(down_hbm.at[:, p], down_ref.at[:, p]) for _, _, p in cut[2 * h : 2 * h + 2]]
    copies += [(gate_pre_hbm, gate_pre_ref), (up_pre_hbm, up_pre_ref)]
    for _, _, p in cut[2:] + cut[:2]:
        copies += [(gate_hbm.at[p, :], gate_ref.at[p, :]), (up_hbm.at[p, :], up_ref.at[p, :])]
    turn = stream(copies, sems)
    hidden_grad = 0.0
    for n, (h, part, p) in enumerate(cut):
        if n % 2 == 0:
            next(turn)
            unpack(arrived[h], rows.at[h])
        next(turn)
        hidden_grad = hidden_grad + dot_last(rows[h, :, part], down_ref[:, p])
    next(turn)
    next(turn)
    activated, slope = silu_parts(gate_pre_ref[...])
    gate_grad = (hidden_grad * up_pre_ref[...] * slope).astype(BF16)
    up_grad = (hidden_grad * activated).astype(BF16)
    for n, (h, part, p) in enumerate(cut[2:] + cut[:2]):
        next(turn)
        product = dot_last(gate_grad, gate_ref[p, :])
        next(turn)
        product = product + dot_last(up_grad, up_ref[p, :])
        pack_quarter(product, part, (out_mine_ref, out_other_ref)[h], n % 2 == 0)


def split_weights_kernel(low, gate_hbm, up_hbm, down_hbm, own_ref, near_ref, gate_ref, up_ref, down_ref, sems):
    for copy in begin(sems, (gate_hbm, gate_ref), (up_hbm, up_ref), (down_hbm, down_ref)):
        copy.wait()
    rest = jnp.zeros((PIECE, DENSE_COLS - 3 * SHARE), F32)
    wide = [ref[...].astype(F32) for ref in (gate_ref, up_ref, down_ref)]
    first = jnp.concatenate([w[:, :SHARE] for w in wide] + [rest], axis=1).astype(BF16)
    second = jnp.concatenate([w[:, SHARE:] for w in wide] + [rest], axis=1).astype(BF16)

    @pl.when(low[0] == 0)
    def _():
        own_ref[...] = first
        near_ref[...] = second

    @pl.when(low[0] != 0)
    def _():
        own_ref[...] = second
        near_ref[...] = first


def dense_kernel(core, *refs):
    own_ref, own_grad_ref, near_m, near_o, *pieces = refs[: 4 + PIECES]
    _, out_mine_ref, out_other_ref, weights, rows, grads, sems = refs[4 + PIECES :]
    at = halves(core)
    near = pl.ds(ROWS, ROWS)
    copies = []

    def copy(source, target):
        copies.append(pltpu.make_async_copy(source, target, sems.at[len(copies)]))
        copies[-1].start()

    copy(own_ref, rows.at[pl.ds(0, ROWS), :])
    copy(own_grad_ref, grads.at[pl.ds(0, ROWS), :])
    for h, ref in enumerate((near_m, near_o)):
        copy(ref.at[pl.ds(0, ROWS), :], rows.at[near, pl.ds(at[h], HALF)])
        copy(ref.at[near, :], grads.at[near, pl.ds(at[h], HALF)])
    for n, (piece, line, *_) in enumerate(PLACES):
        start = pl.multiple_of(core[1 + n], PIECE)
        copy(pieces[piece].at[pl.ds(line, PIECE), :], weights.at[pl.ds(start, PIECE), :])
    for one in copies:
        one.wait()
    pre = dot(rows[...], weights[:, : 2 * SHARE])
    gate_pre, up_pre = pre[:, :SHARE], pre[:, SHARE:]
    hidden_grad = dot(grads[...], weights[:, 512:])[:, 2 * SHARE - 512 : 3 * SHARE - 512]
    activated, slope = silu_parts(gate_pre)
    zeros = lambda n: jnp.zeros((2 * ROWS, n), F32)
    hidden = jnp.concatenate([zeros(2 * SHARE - 512), activated * up_pre, zeros(DENSE_COLS - 3 * SHARE)], axis=1)
    hidden = hidden.astype(BF16)
    pre_grad = jnp.concatenate([hidden_grad * up_pre * slope, hidden_grad * activated], axis=1).astype(BF16)
    for h, ref in ((1, out_other_ref), (0, out_mine_ref)):
        part = pl.ds(at[h], HALF)
        forward = dot_last(hidden, weights[part, 512:]).astype(BF16)
        ref[:ROWS, :] = forward[:ROWS]
        ref[2 * ROWS : 3 * ROWS, :] = forward[ROWS:]
        backward = dot_last(pre_grad, weights[part, : 2 * SHARE]).astype(BF16)
        ref[ROWS : 2 * ROWS, :] = backward[:ROWS]
        ref[3 * ROWS :, :] = backward[ROWS:]


def picked_rows(found, packed):
    first, low, high = found
    rest = packed[:, HALF:]
    return dot(first, packed[:, :HALF]) + jnp.concatenate([dot(low, rest), dot(high, rest)], axis=1)


def thirds(column):
    lanes = lax.broadcasted_iota(I32, (ROWS, 128), 1)
    high = column.astype(BF16).astype(F32)
    middle = (column - high).astype(BF16).astype(F32)
    low = column - high - middle
    return jnp.where(lanes == 0, high, jnp.where(lanes == 1, middle, jnp.where(lanes == 2, low, 0.0))).astype(BF16)


def total(columns):
    return jnp.sum(columns.astype(F32), axis=1, keepdims=True)


def combine(core, routes_ref, back_ref, dense_refs, small_hbm, features_hbm, bufs, sems, first):
    dense, small, features = bufs
    rows = pl.ds(first, ROWS)
    mine = pl.ds(halves(core)[0], HALF)
    sources = [dense_refs[0].at[rows, :], dense_refs[1].at[rows, :], dense_refs[2]]
    copies = begin(
        sems,
        *[(source, dense.at[n]) for n, source in enumerate(sources)],
        (small_hbm, small),
        (features_hbm.at[:, mine], features),
    )
    found = place_marks(routes_of(routes_ref))
    one, two = (picked_rows(found[k], back_ref[...]) for k in range(2))
    for copy in copies:
        copy.wait()
    gate = small[:, 1:2]
    part = dense[0].astype(F32) + dense[1].astype(F32) + dense[2].astype(F32)
    return one, two, part + gate * one + (1.0 - gate) * two


def combine_forward_kernel(
    core, routes_ref, back_ref, dense_a, dense_b, dense_c, small_ref, grad_ref, out_ref, dense, small, grad, sems
):
    one, two, part = combine(
        core, routes_ref, back_ref, (dense_a, dense_b, dense_c), small_ref, grad_ref, (dense, small, grad), sems, 0
    )
    out_ref[:, :HALF] = part.astype(BF16)
    out_ref[:, HALF:] = thirds(jnp.sum(grad[...].astype(F32) * (one - two), axis=1, keepdims=True))


def combine_backward_kernel(
    core, routes_ref, back_ref, dense_a, dense_b, dense_c, small_ref, tokens_ref, gain_ref, out_ref,
    dense, small, tokens, sems,
):
    _, _, part = combine(
        core, routes_ref, back_ref, (dense_a, dense_b, dense_c), small_ref, tokens_ref, (dense, small, tokens), sems, ROWS
    )
    out_ref[:, :HALF] = part.astype(BF16)
    weighted = tokens[...].astype(F32) * gain_ref[:, pl.ds(halves(core)[0], HALF)] * part
    out_ref[:, HALF:] = thirds(jnp.sum(weighted, axis=1, keepdims=True))


def add_far_kernel(core, forward_ref, forward_far_ref, back_ref, back_far_ref, tokens_ref, out_ref):
    layer = tokens_ref[:, pl.ds(halves(core)[0], HALF)].astype(F32) + (
        forward_ref[:, :HALF].astype(F32) + forward_far_ref[:, :HALF].astype(F32)
    )
    out_ref[:ROWS, :HALF] = layer.astype(BF16)
    out_ref[ROWS:, :HALF] = (back_ref[:, :HALF].astype(F32) + back_far_ref[:, :HALF].astype(F32)).astype(BF16)
    out_ref[:ROWS, HALF:] = thirds(total(forward_ref[:, HALF:]) + total(forward_far_ref[:, HALF:]))
    out_ref[ROWS:, HALF:] = thirds(total(back_ref[:, HALF:]) + total(back_far_ref[:, HALF:]))


def finish_kernel(
    core, routes_ref, mine_ref, other_ref, small_ref, tokens_ref, grad_ref, gain_ref, router_ref,
    layer_ref, grad_in_ref,
):
    scale, gate, leaning = small_ref[:, 0:1], small_ref[:, 1:2], small_ref[:, 2:3]
    dots, sums = (
        total(mine_ref[rows, HALF:]) + total(other_ref[rows, HALF:]) for rows in (slice(0, ROWS), slice(ROWS, None))
    )
    logit_grad = gate * (1.0 - gate) * dots
    mean = scale * scale * scale * ((sums + logit_grad * leaning) / D)
    marks = marks_of(routes_of(routes_ref))
    difference = (marks[0] - marks[1]).astype(BF16)
    at = halves(core)
    for h, ref in enumerate((mine_ref, other_ref)):
        part = pl.ds(at[h], HALF)
        layer_ref[:, part] = ref[:ROWS, :HALF]
        grown = ref[ROWS:, :HALF].astype(F32) + logit_grad * dot(difference, router_ref[:, part])
        moved = scale * (grown * gain_ref[:, part]) - tokens_ref[:, part].astype(F32) * mean
        grad_in_ref[:, part] = (grad_ref[:, part].astype(F32) + moved).astype(BF16)


def exchange(packed):
    blocks = packed.reshape(EXPERTS, 8, packed.shape[1])
    return lax.all_to_all(blocks, "expert", split_axis=0, concat_axis=0, tiled=True).reshape(packed.shape)


PIECES = 8


PLACES = [
    (n, (2 * k + side) * PIECE, side, 2 * (n % 2) + k, n // 2)
    for n in range(PIECES)
    for k in range(2)
    for side in range(2)
]


def shards(
    tokens, norm_gain, router, expert_gate, expert_up, expert_down,
    dense_gate, dense_up, dense_down_t, routes, grad_out,
):
    index = lax.axis_index("expert")
    core_index = lax.axis_index("tensor") % 2
    x_lo, y, z = index // 16, (index // 4) % 4, index % 4
    core = core_index.astype(I32).reshape(1)
    gain = norm_gain.reshape(1, D)
    w_gate, w_up, w_down = expert_gate[0], expert_up[0], expert_down[0]

    full = lambda array: (array, False)
    raw = lambda array: (array, True)
    hbm = lambda *shape: (shape, BF16, True)
    kept = lambda *shape: (shape, BF16, False)

    routes = routes.T
    router = router.T

    packed, normed, scale, share = call(
        dispatch_kernel,
        [full(routes), full(tokens), full(gain), full(grad_out)],
        [hbm(LINES, 2 * PACKED), hbm(ROWS, D), ((ROWS, 128), F32, True), hbm(2 * ROWS, HALF)],
        core=core,
        takes=7,
    )

    own_weights, near_weights = call(
        split_weights_kernel,
        [raw(dense_gate), raw(dense_up), raw(dense_down_t)],
        [kept(PIECE, DENSE_COLS)] * 2,
        [pltpu.VMEM((PIECE, HID), BF16)] * 3 + [pltpu.SemaphoreType.DMA((3,))],
        core=x_lo.astype(I32).reshape(1),
    )
    pair = jnp.concatenate([own_weights, send(near_weights, SWAP_XLO)], axis=0)
    packed, pair = lax.optimization_barrier((packed, pair))
    (small,) = call(
        gates_kernel,
        [full(routes), full(tokens), full(gain), full(router), full(normed), full(scale)],
        [((ROWS, 128), F32, True)],
        core=core,
        takes=40,
    )
    arrived, near_mine, small, *around = lax.optimization_barrier(
        (exchange(packed), send(share, TO_X), small, *[send(pair, across(n, True)) for n in (1, 2, 3)])
    )
    low, high = jnp.concatenate([pair, around[0]], axis=0), jnp.concatenate(around[1:], axis=0)
    low_after, high_ahead = send(low, across(1, False)), send(high, across(3, False))
    high_after, low_ahead = send(high, across(1, False)), send(low, across(3, False))

    near_other = send(near_mine, SWAP_CORE)

    arrived_other = send(arrived, SWAP_CORE)
    weights = [raw(w_gate), raw(w_up), raw(w_down)]
    buffers = [pltpu.VMEM((D, HID), BF16), pltpu.VMEM((D, HID), BF16), pltpu.VMEM((HID, D), BF16)]
    buffers += [pltpu.VMEM((SLOTS, HID), F32)] * 2 + [pltpu.VMEM((2, SLOTS, HALF), BF16)]
    result_mine, result_other, gate_pre, up_pre = call(
        expert_forward_kernel,
        [full(arrived), full(arrived_other), *weights],
        [hbm(LINES, PACKED), kept(LINES, PACKED)] + [((SLOTS, HID), F32, "copied")] * 2,
        buffers + [pltpu.SemaphoreType.DMA((8,))],
        core,
        takes=14,
        limit=40,
    )
    result_mine, result_other, low_after, high_ahead, high_after, low_ahead, near_other = lax.optimization_barrier(
        (result_mine, result_other, low_after, high_ahead, high_after, low_ahead, near_other)
    )
    low_far, high_far = send(low_after, across(1, False)), send(high_ahead, across(3, False))

    def joined(mine, other):
        return (mine.astype(F32) + send(other, SWAP_CORE).astype(F32)).astype(BF16)

    result = joined(result_mine, result_other)
    back_result = exchange(result)
    grads_mine, grads_other = call(
        expert_backward_kernel,
        [raw(arrived), raw(arrived_other), raw(gate_pre), raw(up_pre), *weights, raw(result)],
        [hbm(LINES, PACKED), kept(LINES, PACKED)],
        buffers + [pltpu.VMEM((2, LINES, PACKED), BF16), pltpu.SemaphoreType.DMA((16,))],
        core,
        takes=14,
        limit=40,
    )

    def start_of(side, first, second):
        dy, dz = jnp.where(core_index == 0, second, first), jnp.where(core_index == 0, first, second)
        return (((x_lo + side) % 2 * 4 + (y - dy) % 4) * 4 + (z - dz) % 4) * PIECE

    table = jnp.array([place[2:] for place in PLACES], I32)
    starts = start_of(table[:, 0], table[:, 1], table[:, 2]).astype(I32)

    pieces = [low, high, low_after, high_after, low_far, high_far, low_ahead, high_ahead]
    dense_mine, dense_other = call(
        dense_kernel,
        [raw(a) for a in (normed, grad_out, near_mine, near_other, *pieces, grads_other)],
        [hbm(4 * ROWS, HALF), kept(4 * ROWS, HALF)],
        [
            pltpu.VMEM((D, DENSE_COLS), BF16),
            pltpu.VMEM((2 * ROWS, D), BF16),
            pltpu.VMEM((2 * ROWS, D), BF16),
            pltpu.SemaphoreType.DMA((6 + len(PLACES),)),
        ],
        jnp.concatenate([core, starts]),
        takes=12,
        limit=28,
    )
    dense_other, back_result = lax.optimization_barrier((dense_other, back_result))
    dense_far = send(dense_other, SWAP_CORE)
    near_sums = [
        (dense_mine[a : a + ROWS].astype(F32) + dense_far[a : a + ROWS].astype(F32)).astype(BF16)
        for a in (2 * ROWS, 3 * ROWS)
    ]
    grads, *near_sums = lax.optimization_barrier((joined(grads_mine, grads_other), *near_sums))
    back_grads = exchange(grads)

    near_far = [send(near_sum, TO_X) for near_sum in near_sums]

    def dense_part(n):
        return [raw(dense_mine), raw(dense_far), raw(near_far[n])]

    row_buffers = [pltpu.VMEM((3, ROWS, HALF), BF16), pltpu.VMEM((ROWS, 128), F32), pltpu.VMEM((ROWS, HALF), BF16)]
    row_buffers += [pltpu.SemaphoreType.DMA((5,))]
    (forward,) = call(
        combine_forward_kernel,
        [full(routes), full(back_result), *dense_part(0), raw(small), raw(grad_out)],
        [kept(ROWS, HALF + 128)],
        row_buffers,
        core=core,
        takes=9,
    )
    forward, near_far[1] = lax.optimization_barrier((forward, near_far[1]))
    forward_far = send(forward, SWAP_XHI)
    forward, back_grads = lax.optimization_barrier((forward, back_grads))
    (backward,) = call(
        combine_backward_kernel,
        [full(routes), full(back_grads), *dense_part(1), raw(small), raw(tokens), full(gain)],
        [kept(ROWS, HALF + 128)],
        row_buffers,
        core=core,
        takes=1,
    )
    backward, forward_far = lax.optimization_barrier((backward, forward_far))
    backward_far = send(backward, SWAP_XHI)
    (mine,) = call(
        add_far_kernel,
        [full(forward), full(forward_far), full(backward), full(backward_far), full(tokens)],
        [kept(2 * ROWS, HALF + 128)],
        core=core,
    )
    return tuple(
        call(
            finish_kernel,
            [full(routes), full(mine), full(send(mine, SWAP_CORE)), full(small)]
            + [full(tokens), full(grad_out), full(gain), full(router)],
            [kept(ROWS, D)] * 2,
            core=core,
        )
    )


def solution(mesh):
    return jax.shard_map(
        shards,
        mesh=mesh,
        in_specs=(
            P("expert", None),
            P(),
            P(),
            P("expert", None, "tensor"),
            P("expert", None, "tensor"),
            P("expert", "tensor", None),
            P("expert", "tensor"),
            P("expert", "tensor"),
            P("expert", "tensor"),
            P("expert", None),
            P("expert", None),
        ),
        out_specs=(P("expert", None), P("expert", None)),
        check_vma=False,
    )
```
